32 devices in a mesh: gx: 8 (over y, x, core), node: 4 (over z).
Axes of the slice: x: 2, y: 2, z: 4, core: 2. Of those that a mesh axis runs over, the one named last changes fastest.
Arguments:
- logfield: bfloat16 [4, 64, 1024, 256], P('node', 'gx'), may hold values from -4 to 4
- state: float32 [4, 64, 1024, 256], P('node', 'gx'), may hold values from -48 to 48
- target: float32 [64, 1024, 256], P('gx'), may hold values from -48 to 48
- node_index: int32 [4], P('node'), may hold values from 0 to 8
- weight_numer: int32 [4], P('node'), may hold values from 1 to 16
Outputs:
- riesz_gradient: float32 [64, 1024, 256], P('gx', 'node')
The draws below stay inside these ranges and needn't reach their ends.
Inputs may be any that keep to these rules, and one draw needn't show every extreme that they name: `node_index`: index i stands for the abscissa cos(pi i / 8). `weight_numer`: the node's weight is the numerator over 8.
All inputs are finite; a program needn't handle non-finite values.
Results may differ from the reference program's by a relative error of at most 0.0003.
Values may be sent and summed in bfloat16 or wider, within the bound.
A program may use at most 320 MiB of HBM per device.

```python
import math
import jax
import jax.numpy as jnp

NY = 1024
NZ = 256
ADJ_SWEEPS = 2
SMOOTH_SWEEPS = 2
NODES = 4
NX = 64


def set_ends(result, key, least, largest):
    extent = result.shape
    spot = [jax.random.randint(jax.random.fold_in(key, axis), (), 0, extent[axis]) for axis in range(len(extent))]
    result = result.at[tuple(spot)].set(least)
    longest = extent.index(max(extent))
    spot[longest] = (spot[longest] + 1) % extent[longest]
    return result.at[tuple(spot)].set(largest)


def levels(stream_key, dims, shards, low, top_value):
    def one(position, shards_of):
        draws = jax.random.uniform(jax.random.fold_in(jax.random.fold_in(stream_key, 6), position), (shards_of,), jnp.float32, low / len(shards), top_value / len(shards))
        return jnp.repeat(jnp.exp(draws), dims[position] // shards_of).reshape((-1,) + (1,) * (len(dims) - position - 1))

    level = one(*shards[0])
    for cut in shards[1:]:
        level = level * one(*cut)
    return level


def normal_values(own_key, dims, spread, limit, cuts=(), dtype=jnp.bfloat16):
    values = jax.random.normal(own_key, dims, jnp.float32) * spread
    if len(cuts) > 0:
        values = levels(own_key, dims, cuts, -0.22, 0.18) * values
    return jnp.clip(values, min=-limit, max=limit).astype(dtype)


def setup_inputs(seed: int = 0) -> dict:
    arg_keys = jax.random.split(jax.random.key(seed), 6)
    logfield = normal_values(arg_keys[0], (NODES, NX, NY, NZ), 1.0, 4.0, ((0, 4), (1, 8)))
    state = normal_values(arg_keys[1], (NODES, NX, NY, NZ), 8.0, 48.0, ((0, 4), (1, 8)), jnp.float32)
    target = normal_values(arg_keys[2], (NX, NY, NZ), 8.0, 48.0, ((0, 8),), jnp.float32)
    node_index = set_ends(jax.random.randint(arg_keys[3], (NODES,), 0, 9), jax.random.fold_in(arg_keys[3], 1), 0, 8).astype(jnp.int32)
    weight_numer = set_ends(jax.random.randint(arg_keys[4], (NODES,), 1, 17), jax.random.fold_in(arg_keys[4], 1), 1, 16).astype(jnp.int32)
    return dict(logfield=logfield, state=state, target=target, node_index=node_index, weight_numer=weight_numer)


relax = 2.0 / 3.0
riesz_beta = 1.0


def face_terms(kappa_ext):
    center = kappa_ext[1:-1]
    padded_y = jnp.pad(center, ((0, 0), (1, 1), (0, 0)), mode="edge")
    padded_z = jnp.pad(center, ((0, 0), (0, 0), (1, 1)), mode="edge")
    coefs = (0.5 * (center + kappa_ext[:-2]), 0.5 * (center + kappa_ext[2:]),
             0.5 * (center + padded_y[:, :-2]), 0.5 * (center + padded_y[:, 2:]),
             0.5 * (center + padded_z[:, :, :-2]), 0.5 * (center + padded_z[:, :, 2:]))
    diagonal = coefs[0] + coefs[1] + coefs[2] + coefs[3] + coefs[4] + coefs[5]
    return coefs, diagonal


def neighbour_sum(coefs, value_ext):
    center = value_ext[1:-1]
    padded_y = jnp.pad(center, ((0, 0), (1, 1), (0, 0)))
    padded_z = jnp.pad(center, ((0, 0), (0, 0), (1, 1)))
    return (coefs[0] * value_ext[:-2] + coefs[1] * value_ext[2:]
            + coefs[2] * padded_y[:, :-2] + coefs[3] * padded_y[:, 2:]
            + coefs[4] * padded_z[:, :, :-2] + coefs[5] * padded_z[:, :, 2:])


def jacobi_step(previous_ext, misfit, coefs, diagonal):
    center = previous_ext[1:-1]
    image = diagonal * center - neighbour_sum(coefs, previous_ext)
    return center + relax * (misfit - image) / diagonal


def riesz_step(smooth_ext, source):
    center = smooth_ext[1:-1, 1:-1]
    padded_z = jnp.pad(center, ((0, 0), (0, 0), (1, 1)))
    beside_all = (smooth_ext[:-2, 1:-1] + smooth_ext[2:, 1:-1] + smooth_ext[1:-1, :-2]
              + smooth_ext[1:-1, 2:] + padded_z[:, :, :-2] + padded_z[:, :, 2:])
    return (source + riesz_beta * beside_all) / (1.0 + 6.0 * riesz_beta)


def wrap_first(values):
    return jnp.concatenate([values[-1:], values, values[:1]], axis=0)


def reference(logfield, state, target, node_index, weight_numer):
    total = jnp.zeros(target.shape, jnp.float32)
    for node in range(NODES):
        abscissa = jnp.cos(math.pi * node_index[node].astype(jnp.float32) / 8.0)
        kappa = jnp.exp(0.5 * abscissa * logfield[node].astype(jnp.float32))
        coefs, diagonal = face_terms(wrap_first(kappa))
        misfit = state[node] - target
        adjoint = relax * misfit / diagonal
        for sweep in range(ADJ_SWEEPS - 1):
            adjoint = jacobi_step(wrap_first(adjoint), misfit, coefs, diagonal)
        weight = weight_numer[node].astype(jnp.float32) / 8.0
        total = total + weight * adjoint
    smooth = total
    for sweep in range(SMOOTH_SWEEPS):
        smooth_ext = jnp.pad(wrap_first(smooth), ((0, 0), (1, 1), (0, 0)))
        smooth = riesz_step(smooth_ext, total)
    return smooth
```

```python
import functools
import math

import jax
import jax.numpy as jnp
from jax import lax
from jax.experimental import pallas as pl
from jax.experimental.pallas import tpu as pltpu
from jax.sharding import PartitionSpec as P

RELAX = 2.0 / 3.0
BETA = 1.0
TOP = 32767.0
MESH = pl.DeviceIdType.MESH


def rolled(v, by):
    return pltpu.roll(v, by, 1)


def kernel(G, K, X, Y, Z, CH, lf, st, tg, ni, wn, out,
           lfw, stw, tgw, kap, adj, inv, asend, ahalo, term, qs, sc, qr, sr, grad, sm1,
           lf_loc, lf_send, lf_recv, st_sem, tg_sem, a_send, a_recv,
           q_send, q_recv, s_send, s_recv, g_send, g_recv, r_send, r_recv):
    R = Y // K
    C = R // CH
    NC = K * C
    gx = lax.axis_index("gx")
    node = lax.axis_index("node")
    left = lax.rem(gx + G - 1, G)
    right = lax.rem(gx + 1, G)

    barrier = pltpu.get_barrier_semaphore()
    for k in range(K):
        for g in (left, right):
            pl.semaphore_signal(barrier, inc=1, device_id=(g, jnp.int32(k)), device_id_type=MESH)
    for k in range(1, K):
        pl.semaphore_signal(barrier, inc=1, device_id=(gx, lax.rem(node + k, K)), device_id_type=MESH)

    def piece_of(s):
        return lax.rem(node + K - 1 - s // C + K, K)

    def chunk_of(s):
        return piece_of(s) * C + lax.rem(s, C)

    def lf_start(s):
        first = chunk_of(s) * CH
        start = pl.multiple_of(jnp.clip(first - 16, 0, Y - CH - 32), 16)
        dst = pl.multiple_of(32 + start - first, 16)
        return start, dst

    def lf_local(s):
        start, dst = lf_start(s)
        return pltpu.make_async_copy(
            lf.at[0, :, pl.ds(start, CH + 32), :],
            lfw.at[s, pl.ds(1, X), pl.ds(dst, CH + 32), :], lf_loc.at[s])

    def lf_remote(s, side):
        start, dst = lf_start(s)
        src = 0 if side == 1 else X - 1
        to = X + 1 if side == 1 else 0
        return pltpu.make_async_remote_copy(
            src_ref=lf.at[0, src, pl.ds(start, CH + 32), :],
            dst_ref=lfw.at[s, to, pl.ds(dst, CH + 32), :],
            send_sem=lf_send.at[side, s], recv_sem=lf_recv.at[side, s],
            device_id=(left if side == 1 else right, node), device_id_type=MESH)

    def st_copies(s):
        first = chunk_of(s) * CH
        start = pl.multiple_of(jnp.clip(first - 8, 0, Y - CH - 16), 8)
        dst = pl.multiple_of(16 + start - first, 8)
        slot = lax.rem(s, 2)
        return (
            pltpu.make_async_copy(st.at[0, :, pl.ds(start, CH + 16), :],
                                  stw.at[slot, :, pl.ds(dst, CH + 16), :], st_sem.at[slot]),
            pltpu.make_async_copy(tg.at[:, pl.ds(start, CH + 16), :],
                                  tgw.at[slot, :, pl.ds(dst, CH + 16), :], tg_sem.at[slot]))

    def a_remote(s, side):
        return pltpu.make_async_remote_copy(
            src_ref=asend.at[s, 0 if side == 1 else 1],
            dst_ref=ahalo.at[s, side],
            send_sem=a_send.at[side, s], recv_sem=a_recv.at[side, s],
            device_id=(left if side == 1 else right, node), device_id_type=MESH)

    def q_copies(s):
        dest = piece_of(s)
        ci = lax.rem(s, C)
        slot = jnp.where(node < dest, node, node - 1)
        slot = jnp.clip(slot, 0, K - 2)
        return (
            pltpu.make_async_remote_copy(
                src_ref=qs.at[s], dst_ref=qr.at[slot, ci], send_sem=q_send.at[s],
                recv_sem=q_recv.at[slot, ci], device_id=(gx, dest), device_id_type=MESH),
            pltpu.make_async_remote_copy(
                src_ref=sc.at[s], dst_ref=sr.at[slot, ci], send_sem=s_send.at[s],
                recv_sem=s_recv.at[slot, ci], device_id=(gx, dest), device_id_type=MESH))

    index = ni[0]
    half = jnp.float32(0.5 * math.cos(0.0))
    for i in range(1, 9):
        half = jnp.where(index == i, jnp.float32(0.5 * math.cos(math.pi * i / 8)), half)
    weight = wn[0].astype(jnp.float32) / 8.0
    lane = lax.broadcasted_iota(jnp.int32, (16, Z), 1)
    is_first = lane == 0
    is_last = lane == Z - 1

    for s in range(2):
        lf_local(s).start()
    for cp in st_copies(0):
        cp.start()
    pl.semaphore_wait(barrier, 3 * K - 1)
    for s in range(2):
        for side in range(2):
            lf_remote(s, side).start()

    def phase1(s):
        slot = lax.rem(s, 2)
        c = chunk_of(s)

        @pl.when(s + 2 < NC)
        def _():
            lf_local(s + 2).start()
            for side in range(2):
                lf_remote(s + 2, side).start()

        @pl.when(s + 1 < NC)
        def _():
            for cp in st_copies(s + 1):
                cp.start()

        lf_local(s).wait()
        for side in range(2):
            lf_remote(s, side).wait_recv()

        def kappa(p, _):
            for r in range(16, CH + 48, 16):
                kap[slot, p, r:r + 16, :] = jnp.exp(half * lfw[s, p, r:r + 16, :].astype(jnp.float32))
            return 0

        lax.fori_loop(0, X + 2, kappa, 0)

        @pl.when(c == 0)
        def _():
            for p in range(1, X + 1):
                kap[slot, p, 31:32, :] = kap[slot, p, 32:33, :]

        @pl.when(c == NC - 1)
        def _():
            for p in range(1, X + 1):
                kap[slot, p, CH + 32:CH + 33, :] = kap[slot, p, CH + 31:CH + 32, :]

        for cp in st_copies(s):
            cp.wait()

        def first(p, _):
            for r in range(8, CH + 24, 16):
                j = r + 16
                k = kap[slot, p + 1, j:j + 16, :]
                total = (6.0 * k + kap[slot, p, j:j + 16, :] + kap[slot, p + 2, j:j + 16, :]
                         + kap[slot, p + 1, j - 1:j + 15, :] + kap[slot, p + 1, j + 1:j + 17, :]
                         + jnp.where(is_first, k, rolled(k, 1)) + jnp.where(is_last, k, rolled(k, Z - 1)))
                over = 1.0 / total
                inv[slot, p, r:r + 16, :] = over
                adj[slot, p + 1, r:r + 16, :] = (2.0 * RELAX) * (
                    stw[slot, p, r:r + 16, :] - tgw[slot, p, r:r + 16, :]) * over
            return 0

        lax.fori_loop(0, X, first, 0)

        asend[s, 0] = adj[slot, 1, 16:CH + 16, :]
        asend[s, 1] = adj[slot, X, 16:CH + 16, :]
        for side in range(2):
            a_remote(s, side).start()

        @pl.when(c == 0)
        def _():
            for p in range(1, X + 1):
                adj[slot, p, 15:16, :] = jnp.zeros((1, Z), jnp.float32)

        @pl.when(c == NC - 1)
        def _():
            for p in range(1, X + 1):
                adj[slot, p, CH + 16:CH + 17, :] = jnp.zeros((1, Z), jnp.float32)

    def phase2(s):
        slot = lax.rem(s, 2)
        for side in range(2):
            a_remote(s, side).wait_recv()
        adj[slot, 0, 16:CH + 16, :] = ahalo[s, 0]
        adj[slot, X + 1, 16:CH + 16, :] = ahalo[s, 1]

        def second(p, _):
            for r in range(16, CH + 16, 16):
                j = r + 16
                k = kap[slot, p + 1, j:j + 16, :]
                a = adj[slot, p + 1, r:r + 16, :]
                ka = k * a
                am, ap = adj[slot, p, r:r + 16, :], adj[slot, p + 2, r:r + 16, :]
                bm, bp = adj[slot, p + 1, r - 1:r + 15, :], adj[slot, p + 1, r + 1:r + 17, :]
                beside = (am + ap + bm + bp
                          + jnp.where(is_first, 0.0, rolled(a, 1)) + jnp.where(is_last, 0.0, rolled(a, Z - 1)))
                beside_k = (kap[slot, p, j:j + 16, :] * am + kap[slot, p + 2, j:j + 16, :] * ap
                            + kap[slot, p + 1, j - 1:j + 15, :] * bm + kap[slot, p + 1, j + 1:j + 17, :] * bp
                            + jnp.where(is_first, 0.0, rolled(ka, 1)) + jnp.where(is_last, 0.0, rolled(ka, Z - 1)))
                t = (2.0 * RELAX) * weight * a + (RELAX * weight) * (k * beside + beside_k) * inv[slot, p, r:r + 16, :]
                term[p, r - 16:r, :] = t
            return 0

        lax.fori_loop(0, X, second, 0)
        dest = piece_of(s)

        @pl.when(dest == node)
        def _():
            row = pl.multiple_of(8 + lax.rem(s, C) * CH, 8)
            for p in range(X):
                grad[2 + p, pl.ds(row, CH), :] = term[p]

        @pl.when(dest != node)
        def _():
            for g in range(CH // 16):
                most = jnp.abs(term[0, g * 16:g * 16 + 16, :])
                for p in range(1, X):
                    most = jnp.maximum(most, jnp.abs(term[p, g * 16:g * 16 + 16, :]))
                most = jnp.maximum(jnp.max(most, axis=0, keepdims=True), 1e-20)
                sc[s, g:g + 1, :] = most * (1.0 / TOP)
                up = jnp.broadcast_to(TOP / most, (16, Z))
                for p in range(X):
                    q = jnp.round(term[p, g * 16:g * 16 + 16, :] * up)
                    qs[s, p, g * 16:g * 16 + 16, :] = q.astype(jnp.int32).astype(jnp.int16)
            for cp in q_copies(s):
                cp.start()

    def step(s, _):
        @pl.when(s < NC)
        def _():
            phase1(s)

        @pl.when(s >= 1)
        def _():
            phase2(s - 1)

        return 0

    lax.fori_loop(0, NC + 1, step, 0)

    low, high = node == 0, node == K - 1

    def g_remote(ci, side):
        row = pl.multiple_of(8 + ci * CH, 8)
        return pltpu.make_async_remote_copy(
            src_ref=grad.at[pl.ds(2 if side == 1 else X, 2), pl.ds(row, CH), :],
            dst_ref=grad.at[pl.ds(X + 2 if side == 1 else 0, 2), pl.ds(row, CH), :],
            send_sem=g_send.at[side, ci], recv_sem=g_recv.at[side, ci],
            device_id=(left if side == 1 else right, node), device_id_type=MESH)

    def row_copies(up):
        src_row, dst_row, base = (R, 0, 0) if up else (8, R + 8, 3)
        to = jnp.clip(node + (1 if up else -1), 0, K - 1)
        result = []
        for n, (src, dst, count, g) in enumerate((
                (2, 2, X, gx), (2, X + 2, 1, left), (X + 1, 1, 1, right))):
            result.append(pltpu.make_async_remote_copy(
                src_ref=grad.at[pl.ds(src, count), pl.ds(src_row, 8), :],
                dst_ref=grad.at[pl.ds(dst, count), pl.ds(dst_row, 8), :],
                send_sem=r_send.at[base + n], recv_sem=r_recv.at[base + n],
                device_id=(g, to), device_id_type=MESH))
        return result

    def gather(ci, _):
        for j in range(K - 1):
            pltpu.make_async_remote_copy(
                src_ref=qs.at[0], dst_ref=qr.at[j, ci], send_sem=q_send.at[0],
                recv_sem=q_recv.at[j, ci], device_id=(left, node), device_id_type=MESH).wait_recv()
            pltpu.make_async_remote_copy(
                src_ref=sc.at[0], dst_ref=sr.at[j, ci], send_sem=s_send.at[0],
                recv_sem=s_recv.at[j, ci], device_id=(left, node), device_id_type=MESH).wait_recv()

        def plane(p, _):
            for g in range(CH // 16):
                row = pl.multiple_of(8 + ci * CH + g * 16, 8)
                total = grad[2 + p, pl.ds(row, 16), :]
                for j in range(K - 1):
                    total += qr[j, ci, p, g * 16:g * 16 + 16, :].astype(jnp.float32) * sr[j, ci, g:g + 1, :]
                grad[2 + p, pl.ds(row, 16), :] = total
            return 0

        lax.fori_loop(0, X, plane, 0)
        for side in range(2):
            g_remote(ci, side).start()
        return 0

    lax.fori_loop(0, C, gather, 0)

    @pl.when(jnp.logical_not(high))
    def _():
        for cp in row_copies(True):
            cp.start()

    @pl.when(jnp.logical_not(low))
    def _():
        for cp in row_copies(False):
            cp.start()

    @pl.when(low)
    def _():
        grad[:, 0:8, :] = jnp.zeros((X + 4, 8, Z), jnp.float32)

    @pl.when(high)
    def _():
        grad[:, R + 8:R + 16, :] = jnp.zeros((X + 4, 8, Z), jnp.float32)

    @pl.when(jnp.logical_not(low))
    def _():
        for cp in row_copies(True):
            cp.wait_recv()

    @pl.when(jnp.logical_not(high))
    def _():
        for cp in row_copies(False):
            cp.wait_recv()

    def halo_wait(ci, _):
        for side in range(2):
            g_remote(ci, side).wait_recv()
        return 0

    lax.fori_loop(0, C, halo_wait, 0)
    scale = 1.0 / (1.0 + 6.0 * BETA)

    def smoothed(ref, p, source, r, n):
        v = ref[p, r:r + n, :]
        beside = (ref[p - 1, r:r + n, :] + ref[p + 1, r:r + n, :]
                  + ref[p, r - 1:r + n - 1, :] + ref[p, r + 1:r + n + 1, :]
                  + jnp.where(is_first[:n], 0.0, rolled(v, 1)) + jnp.where(is_last[:n], 0.0, rolled(v, Z - 1)))
        return (source + BETA * beside) * scale

    def sweep1(p, _):
        for r in range(8, R + 8, 16):
            sm1[p, r:r + 16, :] = smoothed(grad, p, grad[p, r:r + 16, :], r, 16)
        return 0

    lax.fori_loop(1, X + 3, sweep1, 0)
    keep_low = jnp.where(low, 0.0, 1.0)
    keep_high = jnp.where(high, 0.0, 1.0)

    def sweep1_rows(p, _):
        for r, keep in ((7, keep_low), (R + 8, keep_high)):
            v = grad[p, r:r + 1, :]
            wide = jnp.broadcast_to(v, (8, Z))
            beside = (grad[p - 1, r:r + 1, :] + grad[p + 1, r:r + 1, :]
                      + grad[p, r - 1:r, :] + grad[p, r + 1:r + 2, :]
                      + (jnp.where(is_first[:8], 0.0, rolled(wide, 1))
                         + jnp.where(is_last[:8], 0.0, rolled(wide, Z - 1)))[0:1])
            sm1[p, r:r + 1, :] = (v + BETA * beside) * scale * keep
        return 0

    lax.fori_loop(2, X + 2, sweep1_rows, 0)

    def sweep2(p, _):
        for r in range(8, R + 8, 16):
            out[p - 2, r - 8:r + 8, :] = smoothed(sm1, p, grad[p, r:r + 16, :], r, 16)
        return 0

    lax.fori_loop(2, X + 2, sweep2, 0)

    def drain(s, _):
        for side in range(2):
            lf_remote(s, side).wait_send()
            a_remote(s, side).wait_send()

        @pl.when(piece_of(s) != node)
        def _():
            for cp in q_copies(s):
                cp.wait_send()

        return 0

    lax.fori_loop(0, NC, drain, 0)

    def halo_drain(ci, _):
        for side in range(2):
            g_remote(ci, side).wait_send()
        return 0

    lax.fori_loop(0, C, halo_drain, 0)

    @pl.when(jnp.logical_not(high))
    def _():
        for cp in row_copies(True):
            cp.wait_send()

    @pl.when(jnp.logical_not(low))
    def _():
        for cp in row_copies(False):
            cp.wait_send()


def per_device(G, K, CH, logfield, state, target, node_index, weight_numer):
    X, Y, Z = target.shape
    R = Y // K
    CH = min(CH, R)
    C = R // CH
    NC = K * C
    f32, dma = jnp.float32, pltpu.SemaphoreType.DMA
    anywhere = pl.BlockSpec(memory_space=pl.ANY)
    scalars = pl.BlockSpec(memory_space=pltpu.SMEM)
    return pl.pallas_call(
        functools.partial(kernel, G, K, X, Y, Z, CH),
        out_shape=jax.ShapeDtypeStruct((X, R, Z), f32),
        in_specs=[anywhere, anywhere, anywhere, scalars, scalars],
        out_specs=pl.BlockSpec(memory_space=pltpu.VMEM),
        scratch_shapes=[
            pltpu.VMEM((NC, X + 2, CH + 64, Z), jnp.bfloat16),
            pltpu.VMEM((2, X, CH + 32, Z), f32),
            pltpu.VMEM((2, X, CH + 32, Z), f32),
            pltpu.VMEM((2, X + 2, CH + 64, Z), f32),
            pltpu.VMEM((2, X + 2, CH + 32, Z), f32),
            pltpu.VMEM((2, X, CH + 32, Z), f32),
            pltpu.VMEM((NC, 2, CH, Z), f32),
            pltpu.VMEM((NC, 2, CH, Z), f32),
            pltpu.VMEM((X, CH, Z), f32),
            pltpu.VMEM((NC, X, CH, Z), jnp.int16),
            pltpu.VMEM((NC, 8, Z), f32),
            pltpu.VMEM((K - 1, C, X, CH, Z), jnp.int16),
            pltpu.VMEM((K - 1, C, 8, Z), f32),
            pltpu.VMEM((X + 4, R + 16, Z), f32),
            pltpu.VMEM((X + 4, R + 16, Z), f32),
            dma((NC,)), dma((2, NC)), dma((2, NC)), dma((2,)), dma((2,)), dma((2, NC)), dma((2, NC)),
            dma((NC,)), dma((K - 1, C)), dma((NC,)), dma((K - 1, C)), dma((2, C)), dma((2, C)), dma((6,)), dma((6,)),
        ],
        compiler_params=pltpu.CompilerParams(
            collective_id=0, has_side_effects=True, vmem_limit_bytes=58 * 1024 * 1024),
    )(logfield, state, target, node_index, weight_numer)


def solution(mesh):
    in_specs = (
        P("node", "gx", None, None),
        P("node", "gx", None, None),
        P("gx", None, None),
        P("node"),
        P("node"),
    )
    return jax.shard_map(
        functools.partial(per_device, mesh.shape["gx"], mesh.shape["node"], 64), mesh=mesh,
        in_specs=in_specs, out_specs=P("gx", "node", None), check_vma=False)
```

```python
import functools
import math

import jax
import jax.numpy as jnp
from jax import lax
from jax.experimental import pallas as pl
from jax.experimental.pallas import tpu as pltpu
from jax.sharding import PartitionSpec as P

RELAX = 2.0 / 3.0
BETA = 1.0
TOP = 32767.0
LAG = 2
MESH = pl.DeviceIdType.MESH


def rolled(v, by):
    return pltpu.roll(v, by, 1)


def kernel(G, K, X, Y, Z, CH, lf, st, tg, ni, wn, out,
           lfw, stw, tgw, kap, adj, inv, asend, ahalo, term, qs, sc, qr, sr, grad, sm1,
           lf_loc, lf_send, lf_recv, st_sem, tg_sem, a_send, a_recv,
           q_send, q_recv, s_send, s_recv, g_send, g_recv, r_send, r_recv):
    R = Y // K
    C = R // CH
    NC = K * C
    gx = lax.axis_index("gx")
    node = lax.axis_index("node")
    left = lax.rem(gx + G - 1, G)
    right = lax.rem(gx + 1, G)

    barrier = pltpu.get_barrier_semaphore()
    for k in range(K):
        for g in (left, right):
            pl.semaphore_signal(barrier, inc=1, device_id=(g, jnp.int32(k)), device_id_type=MESH)
    for k in range(1, K):
        pl.semaphore_signal(barrier, inc=1, device_id=(gx, lax.rem(node + k, K)), device_id_type=MESH)

    inner = (node > 0) & (node < K - 1)
    lag = jnp.where(inner, LAG, 0)
    orders = [sorted(range(K), key=lambda d: (-abs(d - p) if d != p else 1, -d)) for p in range(K)]
    turns = []
    for i in range(K):
        turn = jnp.int32(orders[0][i])
        for p in range(1, K):
            turn = jnp.where(node == p, orders[p][i], turn)
        turns.append(turn)

    def piece_of(s):
        i = s // C
        piece = turns[0]
        for n in range(1, K):
            piece = jnp.where(i == n, turns[n], piece)
        return piece

    def chunk_of(s):
        return piece_of(s) * C + lax.rem(s, C)

    def lf_start(s):
        first = chunk_of(s) * CH
        start = pl.multiple_of(jnp.clip(first - 16, 0, Y - CH - 32), 16)
        dst = pl.multiple_of(32 + start - first, 16)
        return start, dst

    def lf_local(s):
        start, dst = lf_start(s)
        return pltpu.make_async_copy(
            lf.at[0, :, pl.ds(start, CH + 32), :],
            lfw.at[s, pl.ds(1, X), pl.ds(dst, CH + 32), :], lf_loc.at[s])

    def lf_remote(s, side):
        start, dst = lf_start(s)
        src = 0 if side == 1 else X - 1
        to = X + 1 if side == 1 else 0
        return pltpu.make_async_remote_copy(
            src_ref=lf.at[0, src, pl.ds(start, CH + 32), :],
            dst_ref=lfw.at[s, to, pl.ds(dst, CH + 32), :],
            send_sem=lf_send.at[side, s], recv_sem=lf_recv.at[side, s],
            device_id=(left if side == 1 else right, node), device_id_type=MESH)

    def st_copies(s):
        first = chunk_of(s) * CH
        start = pl.multiple_of(jnp.clip(first - 8, 0, Y - CH - 16), 8)
        dst = pl.multiple_of(16 + start - first, 8)
        slot = lax.rem(s, 2)
        return (
            pltpu.make_async_copy(st.at[0, :, pl.ds(start, CH + 16), :],
                                  stw.at[slot, :, pl.ds(dst, CH + 16), :], st_sem.at[slot]),
            pltpu.make_async_copy(tg.at[:, pl.ds(start, CH + 16), :],
                                  tgw.at[slot, :, pl.ds(dst, CH + 16), :], tg_sem.at[slot]))

    def a_remote(s, side):
        return pltpu.make_async_remote_copy(
            src_ref=asend.at[s, 0 if side == 1 else 1],
            dst_ref=ahalo.at[s, side],
            send_sem=a_send.at[side, s], recv_sem=a_recv.at[side, s],
            device_id=(left if side == 1 else right, node), device_id_type=MESH)

    def q_copies(s):
        dest = piece_of(s)
        ci = lax.rem(s, C)
        upward = dest > node
        slot = jnp.where(dest == node - 1, K, dest)
        to = jnp.clip(jnp.where(upward, node + 1, node - 1), 0, K - 1)
        return (
            pltpu.make_async_remote_copy(
                src_ref=qs.at[s], dst_ref=qr.at[slot, ci], send_sem=q_send.at[s],
                recv_sem=q_recv.at[slot, ci], device_id=(gx, to), device_id_type=MESH),
            pltpu.make_async_remote_copy(
                src_ref=sc.at[s], dst_ref=sr.at[slot, ci], send_sem=s_send.at[s],
                recv_sem=s_recv.at[slot, ci], device_id=(gx, to), device_id_type=MESH))

    index = ni[0]
    half = jnp.float32(0.5 * math.cos(0.0))
    for i in range(1, 9):
        half = jnp.where(index == i, jnp.float32(0.5 * math.cos(math.pi * i / 8)), half)
    weight = wn[0].astype(jnp.float32) / 8.0
    lane = lax.broadcasted_iota(jnp.int32, (16, Z), 1)
    is_first = lane == 0
    is_last = lane == Z - 1

    for s in range(2):
        lf_local(s).start()
    for cp in st_copies(0):
        cp.start()
    pl.semaphore_wait(barrier, 3 * K - 1)
    for s in range(2):
        for side in range(2):
            lf_remote(s, side).start()

    def arrived(slot, ci):
        pltpu.make_async_remote_copy(
            src_ref=qs.at[0], dst_ref=qr.at[slot, ci], send_sem=q_send.at[0],
            recv_sem=q_recv.at[slot, ci], device_id=(left, node), device_id_type=MESH).wait_recv()
        pltpu.make_async_remote_copy(
            src_ref=sc.at[0], dst_ref=sr.at[slot, ci], send_sem=s_send.at[0],
            recv_sem=s_recv.at[slot, ci], device_id=(left, node), device_id_type=MESH).wait_recv()

    def phase1(s):
        slot = lax.rem(s, 2)
        c = chunk_of(s)

        @pl.when(s + 2 < NC)
        def _():
            lf_local(s + 2).start()
            for side in range(2):
                lf_remote(s + 2, side).start()

        @pl.when(s + 1 < NC)
        def _():
            for cp in st_copies(s + 1):
                cp.start()

        lf_local(s).wait()
        for side in range(2):
            lf_remote(s, side).wait_recv()

        def kappa(p, _):
            for r in range(16, CH + 48, 16):
                kap[slot, p, r:r + 16, :] = jnp.exp(half * lfw[s, p, r:r + 16, :].astype(jnp.float32))
            return 0

        lax.fori_loop(0, X + 2, kappa, 0)

        @pl.when(c == 0)
        def _():
            for p in range(1, X + 1):
                kap[slot, p, 31:32, :] = kap[slot, p, 32:33, :]

        @pl.when(c == NC - 1)
        def _():
            for p in range(1, X + 1):
                kap[slot, p, CH + 32:CH + 33, :] = kap[slot, p, CH + 31:CH + 32, :]

        for cp in st_copies(s):
            cp.wait()

        def first(p, _):
            for r in range(8, CH + 24, 16):
                j = r + 16
                k = kap[slot, p + 1, j:j + 16, :]
                total = (6.0 * k + kap[slot, p, j:j + 16, :] + kap[slot, p + 2, j:j + 16, :]
                         + kap[slot, p + 1, j - 1:j + 15, :] + kap[slot, p + 1, j + 1:j + 17, :]
                         + jnp.where(is_first, k, rolled(k, 1)) + jnp.where(is_last, k, rolled(k, Z - 1)))
                over = 1.0 / total
                inv[slot, p, r:r + 16, :] = over
                adj[slot, p + 1, r:r + 16, :] = (2.0 * RELAX) * (
                    stw[slot, p, r:r + 16, :] - tgw[slot, p, r:r + 16, :]) * over
            return 0

        lax.fori_loop(0, X, first, 0)

        asend[s, 0] = adj[slot, 1, 16:CH + 16, :]
        asend[s, 1] = adj[slot, X, 16:CH + 16, :]
        for side in range(2):
            a_remote(s, side).start()

        @pl.when(c == 0)
        def _():
            for p in range(1, X + 1):
                adj[slot, p, 15:16, :] = jnp.zeros((1, Z), jnp.float32)

        @pl.when(c == NC - 1)
        def _():
            for p in range(1, X + 1):
                adj[slot, p, CH + 16:CH + 17, :] = jnp.zeros((1, Z), jnp.float32)

    def phase2(s):
        slot = lax.rem(s, 2)
        place = lax.rem(s, LAG + 1)
        for side in range(2):
            a_remote(s, side).wait_recv()
        adj[slot, 0, 16:CH + 16, :] = ahalo[s, 0]
        adj[slot, X + 1, 16:CH + 16, :] = ahalo[s, 1]

        def second(p, _):
            for r in range(16, CH + 16, 16):
                j = r + 16
                k = kap[slot, p + 1, j:j + 16, :]
                a = adj[slot, p + 1, r:r + 16, :]
                ka = k * a
                am, ap = adj[slot, p, r:r + 16, :], adj[slot, p + 2, r:r + 16, :]
                bm, bp = adj[slot, p + 1, r - 1:r + 15, :], adj[slot, p + 1, r + 1:r + 17, :]
                beside = (am + ap + bm + bp
                          + jnp.where(is_first, 0.0, rolled(a, 1)) + jnp.where(is_last, 0.0, rolled(a, Z - 1)))
                beside_k = (kap[slot, p, j:j + 16, :] * am + kap[slot, p + 2, j:j + 16, :] * ap
                            + kap[slot, p + 1, j - 1:j + 15, :] * bm + kap[slot, p + 1, j + 1:j + 17, :] * bp
                            + jnp.where(is_first, 0.0, rolled(ka, 1)) + jnp.where(is_last, 0.0, rolled(ka, Z - 1)))
                t = (2.0 * RELAX) * weight * a + (RELAX * weight) * (k * beside + beside_k) * inv[slot, p, r:r + 16, :]
                term[place, p, r - 16:r, :] = t
            return 0

        lax.fori_loop(0, X, second, 0)

    def phase3(s):
        place = lax.rem(s, LAG + 1)
        dest = piece_of(s)
        ci = lax.rem(s, C)

        @pl.when((dest != node) & inner)
        def _():
            arrived(dest, ci)

            def add(p, _):
                for g in range(CH // 16):
                    rows = slice(g * 16, g * 16 + 16)
                    term[place, p, rows, :] += qr[dest, ci, p, rows, :].astype(jnp.float32) * sr[dest, ci, g:g + 1, :]
                return 0

            lax.fori_loop(0, X, add, 0)

        @pl.when(dest == node)
        def _():
            row = pl.multiple_of(8 + lax.rem(s, C) * CH, 8)
            for p in range(X):
                grad[2 + p, pl.ds(row, CH), :] = term[place, p]

        @pl.when(dest != node)
        def _():
            for g in range(CH // 16):
                most = jnp.abs(term[place, 0, g * 16:g * 16 + 16, :])
                for p in range(1, X):
                    most = jnp.maximum(most, jnp.abs(term[place, p, g * 16:g * 16 + 16, :]))
                most = jnp.maximum(jnp.max(most, axis=0, keepdims=True), 1e-20)
                sc[s, g:g + 1, :] = most * (1.0 / TOP)
                up = jnp.broadcast_to(TOP / most, (16, Z))
                for p in range(X):
                    q = jnp.round(term[place, p, g * 16:g * 16 + 16, :] * up)
                    qs[s, p, g * 16:g * 16 + 16, :] = q.astype(jnp.int32).astype(jnp.int16)
            for cp in q_copies(s):
                cp.start()

    def step(s, _):
        @pl.when(s < NC)
        def _():
            phase1(s)

        @pl.when((s >= 1) & (s < NC + 1))
        def _():
            phase2(s - 1)

        @pl.when((s >= 1 + lag) & (s < NC + 1 + lag))
        def _():
            phase3(s - 1 - lag)

        return 0

    lax.fori_loop(0, NC + 1 + LAG, step, 0)

    low, high = node == 0, node == K - 1

    def g_remote(ci, side):
        row = pl.multiple_of(8 + ci * CH, 8)
        return pltpu.make_async_remote_copy(
            src_ref=grad.at[pl.ds(2 if side == 1 else X, 2), pl.ds(row, CH), :],
            dst_ref=grad.at[pl.ds(X + 2 if side == 1 else 0, 2), pl.ds(row, CH), :],
            send_sem=g_send.at[side, ci], recv_sem=g_recv.at[side, ci],
            device_id=(left if side == 1 else right, node), device_id_type=MESH)

    def row_copies(up):
        src_row, dst_row, base = (R, 0, 0) if up else (8, R + 8, 3)
        to = jnp.clip(node + (1 if up else -1), 0, K - 1)
        result = []
        for n, (src, dst, count, g) in enumerate((
                (2, 2, X, gx), (2, X + 2, 1, left), (X + 1, 1, 1, right))):
            result.append(pltpu.make_async_remote_copy(
                src_ref=grad.at[pl.ds(src, count), pl.ds(src_row, 8), :],
                dst_ref=grad.at[pl.ds(dst, count), pl.ds(dst_row, 8), :],
                send_sem=r_send.at[base + n], recv_sem=r_recv.at[base + n],
                device_id=(g, to), device_id_type=MESH))
        return result

    def gather(ci, _):
        def add(slot):
            arrived(slot, ci)

            def plane(p, _):
                for g in range(CH // 16):
                    row = pl.multiple_of(8 + ci * CH + g * 16, 8)
                    grad[2 + p, pl.ds(row, 16), :] += (
                        qr[slot, ci, p, g * 16:g * 16 + 16, :].astype(jnp.float32) * sr[slot, ci, g:g + 1, :])
                return 0

            lax.fori_loop(0, X, plane, 0)

        @pl.when(node > 0)
        def _():
            add(node)

        @pl.when(node < K - 1)
        def _():
            add(jnp.int32(K))

        for side in range(2):
            g_remote(ci, side).start()
        return 0

    lax.fori_loop(0, C, gather, 0)

    @pl.when(jnp.logical_not(high))
    def _():
        for cp in row_copies(True):
            cp.start()

    @pl.when(jnp.logical_not(low))
    def _():
        for cp in row_copies(False):
            cp.start()

    @pl.when(low)
    def _():
        grad[:, 0:8, :] = jnp.zeros((X + 4, 8, Z), jnp.float32)

    @pl.when(high)
    def _():
        grad[:, R + 8:R + 16, :] = jnp.zeros((X + 4, 8, Z), jnp.float32)

    @pl.when(jnp.logical_not(low))
    def _():
        for cp in row_copies(True):
            cp.wait_recv()

    @pl.when(jnp.logical_not(high))
    def _():
        for cp in row_copies(False):
            cp.wait_recv()

    def halo_wait(ci, _):
        for side in range(2):
            g_remote(ci, side).wait_recv()
        return 0

    lax.fori_loop(0, C, halo_wait, 0)
    scale = 1.0 / (1.0 + 6.0 * BETA)

    def smoothed(ref, p, source, r, n):
        v = ref[p, r:r + n, :]
        beside = (ref[p - 1, r:r + n, :] + ref[p + 1, r:r + n, :]
                  + ref[p, r - 1:r + n - 1, :] + ref[p, r + 1:r + n + 1, :]
                  + jnp.where(is_first[:n], 0.0, rolled(v, 1)) + jnp.where(is_last[:n], 0.0, rolled(v, Z - 1)))
        return (source + BETA * beside) * scale

    def sweep1(p, _):
        for r in range(8, R + 8, 16):
            sm1[p, r:r + 16, :] = smoothed(grad, p, grad[p, r:r + 16, :], r, 16)
        return 0

    lax.fori_loop(1, X + 3, sweep1, 0)
    keep_low = jnp.where(low, 0.0, 1.0)
    keep_high = jnp.where(high, 0.0, 1.0)

    def sweep1_rows(p, _):
        for r, keep in ((7, keep_low), (R + 8, keep_high)):
            v = grad[p, r:r + 1, :]
            wide = jnp.broadcast_to(v, (8, Z))
            beside = (grad[p - 1, r:r + 1, :] + grad[p + 1, r:r + 1, :]
                      + grad[p, r - 1:r, :] + grad[p, r + 1:r + 2, :]
                      + (jnp.where(is_first[:8], 0.0, rolled(wide, 1))
                         + jnp.where(is_last[:8], 0.0, rolled(wide, Z - 1)))[0:1])
            sm1[p, r:r + 1, :] = (v + BETA * beside) * scale * keep
        return 0

    lax.fori_loop(2, X + 2, sweep1_rows, 0)

    def sweep2(p, _):
        for r in range(8, R + 8, 16):
            out[p - 2, r - 8:r + 8, :] = smoothed(sm1, p, grad[p, r:r + 16, :], r, 16)
        return 0

    lax.fori_loop(2, X + 2, sweep2, 0)

    def drain(s, _):
        for side in range(2):
            lf_remote(s, side).wait_send()
            a_remote(s, side).wait_send()

        @pl.when(piece_of(s) != node)
        def _():
            for cp in q_copies(s):
                cp.wait_send()

        return 0

    lax.fori_loop(0, NC, drain, 0)

    def halo_drain(ci, _):
        for side in range(2):
            g_remote(ci, side).wait_send()
        return 0

    lax.fori_loop(0, C, halo_drain, 0)

    @pl.when(jnp.logical_not(high))
    def _():
        for cp in row_copies(True):
            cp.wait_send()

    @pl.when(jnp.logical_not(low))
    def _():
        for cp in row_copies(False):
            cp.wait_send()


def per_device(G, K, CH, logfield, state, target, node_index, weight_numer):
    X, Y, Z = target.shape
    R = Y // K
    CH = min(CH, R)
    C = R // CH
    NC = K * C
    f32, dma = jnp.float32, pltpu.SemaphoreType.DMA
    anywhere = pl.BlockSpec(memory_space=pl.ANY)
    scalars = pl.BlockSpec(memory_space=pltpu.SMEM)
    return pl.pallas_call(
        functools.partial(kernel, G, K, X, Y, Z, CH),
        out_shape=jax.ShapeDtypeStruct((X, R, Z), f32),
        in_specs=[anywhere, anywhere, anywhere, scalars, scalars],
        out_specs=pl.BlockSpec(memory_space=pltpu.VMEM),
        scratch_shapes=[
            pltpu.VMEM((NC, X + 2, CH + 64, Z), jnp.bfloat16),
            pltpu.VMEM((2, X, CH + 32, Z), f32),
            pltpu.VMEM((2, X, CH + 32, Z), f32),
            pltpu.VMEM((2, X + 2, CH + 64, Z), f32),
            pltpu.VMEM((2, X + 2, CH + 32, Z), f32),
            pltpu.VMEM((2, X, CH + 32, Z), f32),
            pltpu.VMEM((NC, 2, CH, Z), f32),
            pltpu.VMEM((NC, 2, CH, Z), f32),
            pltpu.VMEM((LAG + 1, X, CH, Z), f32),
            pltpu.VMEM((NC, X, CH, Z), jnp.int16),
            pltpu.VMEM((NC, 8, Z), f32),
            pltpu.VMEM((K + 1, C, X, CH, Z), jnp.int16),
            pltpu.VMEM((K + 1, C, 8, Z), f32),
            pltpu.VMEM((X + 4, R + 16, Z), f32),
            pltpu.VMEM((X + 4, R + 16, Z), f32),
            dma((NC,)), dma((2, NC)), dma((2, NC)), dma((2,)), dma((2,)), dma((2, NC)), dma((2, NC)),
            dma((NC,)), dma((K + 1, C)), dma((NC,)), dma((K + 1, C)), dma((2, C)), dma((2, C)), dma((6,)), dma((6,)),
        ],
        compiler_params=pltpu.CompilerParams(
            collective_id=0, has_side_effects=True, vmem_limit_bytes=58 * 1024 * 1024),
    )(logfield, state, target, node_index, weight_numer)


def solution(mesh):
    in_specs = (
        P("node", "gx", None, None),
        P("node", "gx", None, None),
        P("gx", None, None),
        P("node"),
        P("node"),
    )
    return jax.shard_map(
        functools.partial(per_device, mesh.shape["gx"], mesh.shape["node"], 64), mesh=mesh,
        in_specs=in_specs, out_specs=P("gx", "node", None), check_vma=False)
```

```python
import functools
import math

import jax
import jax.numpy as jnp
from jax import lax
from jax.experimental import pallas as pl
from jax.experimental.pallas import tpu as pltpu
from jax.sharding import PartitionSpec as P

RELAX = 2.0 / 3.0
BETA = 1.0
TOP = 32767.0
LAG = 2
MESH = pl.DeviceIdType.MESH


def rolled(v, by):
    return pltpu.roll(v, by, 1)


def kernel(G, K, X, Y, Z, CH, lf, st, tg, ni, wn, out,
           lfw, stw, tgw, kap, adj, inv, asend, ahalo, term, qs, sc, qr, sr, grad, sm1,
           lf_loc, lf_send, lf_recv, st_sem, tg_sem, a_send, a_recv,
           q_send, q_recv, s_send, s_recv, g_send, g_recv, r_send, r_recv):
    R = Y // K
    C = R // CH
    NC = K * C
    gx = lax.axis_index("gx")
    node = lax.axis_index("node")
    left = lax.rem(gx + G - 1, G)
    right = lax.rem(gx + 1, G)

    barrier = pltpu.get_barrier_semaphore()
    for k in range(K):
        for g in (left, right):
            pl.semaphore_signal(barrier, inc=1, device_id=(g, jnp.int32(k)), device_id_type=MESH)
    for k in range(1, K):
        pl.semaphore_signal(barrier, inc=1, device_id=(gx, lax.rem(node + k, K)), device_id_type=MESH)

    inner = (node > 0) & (node < K - 1)
    lag = jnp.where(inner, LAG, 0)
    orders = [sorted(range(K), key=lambda d: (-abs(d - p) if d != p else 1, -d)) for p in range(K)]
    turns = []
    for i in range(K):
        turn = jnp.int32(orders[0][i])
        for p in range(1, K):
            turn = jnp.where(node == p, orders[p][i], turn)
        turns.append(turn)

    def piece_of(s):
        i = s // C
        piece = turns[0]
        for n in range(1, K):
            piece = jnp.where(i == n, turns[n], piece)
        return piece

    def chunk_of(s):
        return piece_of(s) * C + lax.rem(s, C)

    def lf_start(s):
        first = chunk_of(s) * CH
        start = pl.multiple_of(jnp.clip(first - 16, 0, Y - CH - 32), 16)
        dst = pl.multiple_of(32 + start - first, 16)
        return start, dst

    def lf_local(s):
        start, dst = lf_start(s)
        return pltpu.make_async_copy(
            lf.at[0, :, pl.ds(start, CH + 32), :],
            lfw.at[s, pl.ds(1, X), pl.ds(dst, CH + 32), :], lf_loc.at[s])

    def lf_remote(s, side):
        start, dst = lf_start(s)
        src = 0 if side == 1 else X - 1
        to = X + 1 if side == 1 else 0
        return pltpu.make_async_remote_copy(
            src_ref=lf.at[0, src, pl.ds(start, CH + 32), :],
            dst_ref=lfw.at[s, to, pl.ds(dst, CH + 32), :],
            send_sem=lf_send.at[side, s], recv_sem=lf_recv.at[side, s],
            device_id=(left if side == 1 else right, node), device_id_type=MESH)

    def st_copies(s):
        first = chunk_of(s) * CH
        start = pl.multiple_of(jnp.clip(first - 8, 0, Y - CH - 16), 8)
        dst = pl.multiple_of(16 + start - first, 8)
        slot = lax.rem(s, 2)
        return (
            pltpu.make_async_copy(st.at[0, :, pl.ds(start, CH + 16), :],
                                  stw.at[slot, :, pl.ds(dst, CH + 16), :], st_sem.at[slot]),
            pltpu.make_async_copy(tg.at[:, pl.ds(start, CH + 16), :],
                                  tgw.at[slot, :, pl.ds(dst, CH + 16), :], tg_sem.at[slot]))

    def a_remote(s, side):
        return pltpu.make_async_remote_copy(
            src_ref=asend.at[s, 0 if side == 1 else 1],
            dst_ref=ahalo.at[s, side],
            send_sem=a_send.at[side, s], recv_sem=a_recv.at[side, s],
            device_id=(left if side == 1 else right, node), device_id_type=MESH)

    def q_copies(s):
        dest = piece_of(s)
        ci = lax.rem(s, C)
        upward = dest > node
        slot = jnp.where(dest == node - 1, K, dest)
        to = jnp.clip(jnp.where(upward, node + 1, node - 1), 0, K - 1)
        return (
            pltpu.make_async_remote_copy(
                src_ref=qs.at[s], dst_ref=qr.at[slot, ci], send_sem=q_send.at[s],
                recv_sem=q_recv.at[slot, ci], device_id=(gx, to), device_id_type=MESH),
            pltpu.make_async_remote_copy(
                src_ref=sc.at[s], dst_ref=sr.at[slot, ci], send_sem=s_send.at[s],
                recv_sem=s_recv.at[slot, ci], device_id=(gx, to), device_id_type=MESH))

    index = ni[0]
    half = jnp.float32(0.5 * math.cos(0.0))
    for i in range(1, 9):
        half = jnp.where(index == i, jnp.float32(0.5 * math.cos(math.pi * i / 8)), half)
    weight = wn[0].astype(jnp.float32) / 8.0
    lane = lax.broadcasted_iota(jnp.int32, (16, Z), 1)
    is_first = lane == 0
    is_last = lane == Z - 1

    for s in range(2):
        lf_local(s).start()
    for cp in st_copies(0):
        cp.start()
    pl.semaphore_wait(barrier, 3 * K - 1)
    for s in range(2):
        for side in range(2):
            lf_remote(s, side).start()

    def arrived(slot, ci):
        pltpu.make_async_remote_copy(
            src_ref=qs.at[0], dst_ref=qr.at[slot, ci], send_sem=q_send.at[0],
            recv_sem=q_recv.at[slot, ci], device_id=(left, node), device_id_type=MESH).wait_recv()
        pltpu.make_async_remote_copy(
            src_ref=sc.at[0], dst_ref=sr.at[slot, ci], send_sem=s_send.at[0],
            recv_sem=s_recv.at[slot, ci], device_id=(left, node), device_id_type=MESH).wait_recv()

    def phase1(s):
        slot = lax.rem(s, 2)
        c = chunk_of(s)

        @pl.when(s + 2 < NC)
        def _():
            lf_local(s + 2).start()
            for side in range(2):
                lf_remote(s + 2, side).start()

        @pl.when(s + 1 < NC)
        def _():
            for cp in st_copies(s + 1):
                cp.start()

        lf_local(s).wait()
        for side in range(2):
            lf_remote(s, side).wait_recv()

        def kappa(p, _):
            for r in range(16, CH + 48, 16):
                kap[slot, p, r:r + 16, :] = jnp.exp(half * lfw[s, p, r:r + 16, :].astype(jnp.float32))
            return 0

        lax.fori_loop(0, X + 2, kappa, 0)

        @pl.when(c == 0)
        def _():
            for p in range(1, X + 1):
                kap[slot, p, 31:32, :] = kap[slot, p, 32:33, :]

        @pl.when(c == NC - 1)
        def _():
            for p in range(1, X + 1):
                kap[slot, p, CH + 32:CH + 33, :] = kap[slot, p, CH + 31:CH + 32, :]

        for cp in st_copies(s):
            cp.wait()

        def first(p, _):
            for r in range(8, CH + 24, 16):
                j = r + 16
                k = kap[slot, p + 1, j:j + 16, :]
                total = (6.0 * k + kap[slot, p, j:j + 16, :] + kap[slot, p + 2, j:j + 16, :]
                         + kap[slot, p + 1, j - 1:j + 15, :] + kap[slot, p + 1, j + 1:j + 17, :]
                         + jnp.where(is_first, k, rolled(k, 1)) + jnp.where(is_last, k, rolled(k, Z - 1)))
                over = 1.0 / total
                inv[slot, p, r:r + 16, :] = over
                adj[slot, p + 1, r:r + 16, :] = (2.0 * RELAX) * (
                    stw[slot, p, r:r + 16, :] - tgw[slot, p, r:r + 16, :]) * over
            return 0

        lax.fori_loop(0, X, first, 0)

        asend[s, 0] = adj[slot, 1, 16:CH + 16, :]
        asend[s, 1] = adj[slot, X, 16:CH + 16, :]
        for side in range(2):
            a_remote(s, side).start()

        @pl.when(c == 0)
        def _():
            for p in range(1, X + 1):
                adj[slot, p, 15:16, :] = jnp.zeros((1, Z), jnp.float32)

        @pl.when(c == NC - 1)
        def _():
            for p in range(1, X + 1):
                adj[slot, p, CH + 16:CH + 17, :] = jnp.zeros((1, Z), jnp.float32)

    def phase2(s):
        slot = lax.rem(s, 2)
        place = lax.rem(s, LAG + 1)
        for side in range(2):
            a_remote(s, side).wait_recv()
        adj[slot, 0, 16:CH + 16, :] = ahalo[s, 0]
        adj[slot, X + 1, 16:CH + 16, :] = ahalo[s, 1]

        def second(p, _):
            for r in range(16, CH + 16, 16):
                j = r + 16
                k = kap[slot, p + 1, j:j + 16, :]
                a = adj[slot, p + 1, r:r + 16, :]
                ka = k * a
                am, ap = adj[slot, p, r:r + 16, :], adj[slot, p + 2, r:r + 16, :]
                bm, bp = adj[slot, p + 1, r - 1:r + 15, :], adj[slot, p + 1, r + 1:r + 17, :]
                beside = (am + ap + bm + bp
                          + jnp.where(is_first, 0.0, rolled(a, 1)) + jnp.where(is_last, 0.0, rolled(a, Z - 1)))
                beside_k = (kap[slot, p, j:j + 16, :] * am + kap[slot, p + 2, j:j + 16, :] * ap
                            + kap[slot, p + 1, j - 1:j + 15, :] * bm + kap[slot, p + 1, j + 1:j + 17, :] * bp
                            + jnp.where(is_first, 0.0, rolled(ka, 1)) + jnp.where(is_last, 0.0, rolled(ka, Z - 1)))
                t = (2.0 * RELAX) * weight * a + (RELAX * weight) * (k * beside + beside_k) * inv[slot, p, r:r + 16, :]
                term[place, p, r - 16:r, :] = t
            return 0

        lax.fori_loop(0, X, second, 0)

    def phase3(s):
        place = lax.rem(s, LAG + 1)
        dest = piece_of(s)
        ci = lax.rem(s, C)

        @pl.when((dest != node) & inner)
        def _():
            arrived(dest, ci)

            def add(p, _):
                for g in range(CH // 16):
                    rows = slice(g * 16, g * 16 + 16)
                    term[place, p, rows, :] += qr[dest, ci, p, rows, :].astype(jnp.float32) * sr[dest, ci, g:g + 1, :]
                return 0

            lax.fori_loop(0, X, add, 0)

        @pl.when(dest == node)
        def _():
            row = pl.multiple_of(8 + lax.rem(s, C) * CH, 8)
            for p in range(X):
                grad[2 + p, pl.ds(row, CH), :] = term[place, p]

        @pl.when(dest != node)
        def _():
            for g in range(CH // 16):
                most = jnp.abs(term[place, 0, g * 16:g * 16 + 16, :])
                for p in range(1, X):
                    most = jnp.maximum(most, jnp.abs(term[place, p, g * 16:g * 16 + 16, :]))
                most = jnp.maximum(jnp.max(most, axis=0, keepdims=True), 1e-20)
                sc[s, g:g + 1, :] = most * (1.0 / TOP)
                up = jnp.broadcast_to(TOP / most, (16, Z))
                for p in range(X):
                    q = jnp.round(term[place, p, g * 16:g * 16 + 16, :] * up)
                    qs[s, p, g * 16:g * 16 + 16, :] = q.astype(jnp.int32).astype(jnp.int16)
            for cp in q_copies(s):
                cp.start()

    def step(s, _):
        @pl.when(s < NC)
        def _():
            phase1(s)

        @pl.when((s >= 1) & (s < NC + 1))
        def _():
            phase2(s - 1)

        @pl.when((s >= 1 + lag) & (s < NC + 1 + lag))
        def _():
            phase3(s - 1 - lag)

        return 0

    lax.fori_loop(0, NC + 1 + LAG, step, 0)

    low, high = node == 0, node == K - 1

    def g_remote(ci, side):
        row = pl.multiple_of(8 + ci * CH, 8)
        return pltpu.make_async_remote_copy(
            src_ref=grad.at[pl.ds(2 if side == 1 else X, 2), pl.ds(row, CH), :],
            dst_ref=grad.at[pl.ds(X + 2 if side == 1 else 0, 2), pl.ds(row, CH), :],
            send_sem=g_send.at[side, ci], recv_sem=g_recv.at[side, ci],
            device_id=(left if side == 1 else right, node), device_id_type=MESH)

    def row_copies(up):
        src_row, dst_row, base = (R, 0, 0) if up else (8, R + 8, 3)
        to = jnp.clip(node + (1 if up else -1), 0, K - 1)
        result = []
        for n, (src, dst, count, g) in enumerate((
                (2, 2, X, gx), (2, X + 2, 1, left), (X + 1, 1, 1, right))):
            result.append(pltpu.make_async_remote_copy(
                src_ref=grad.at[pl.ds(src, count), pl.ds(src_row, 8), :],
                dst_ref=grad.at[pl.ds(dst, count), pl.ds(dst_row, 8), :],
                send_sem=r_send.at[base + n], recv_sem=r_recv.at[base + n],
                device_id=(g, to), device_id_type=MESH))
        return result

    def gather(ci):
        def add(slot):
            arrived(slot, ci)

            def plane(p, _):
                for g in range(CH // 16):
                    row = pl.multiple_of(8 + ci * CH + g * 16, 8)
                    grad[2 + p, pl.ds(row, 16), :] += (
                        qr[slot, ci, p, g * 16:g * 16 + 16, :].astype(jnp.float32) * sr[slot, ci, g:g + 1, :])
                return 0

            lax.fori_loop(0, X, plane, 0)

        @pl.when(node > 0)
        def _():
            add(node)

        @pl.when(node < K - 1)
        def _():
            add(jnp.int32(K))

        for side in range(2):
            g_remote(ci, side).start()

    scale = 1.0 / (1.0 + 6.0 * BETA)

    def smoothed(ref, p, source, r, n):
        v = ref[p, r:r + n, :]
        beside = (ref[p - 1, r:r + n, :] + ref[p + 1, r:r + n, :]
                  + ref[p, r - 1:r + n - 1, :] + ref[p, r + 1:r + n + 1, :]
                  + jnp.where(is_first[:n], 0.0, rolled(v, 1)) + jnp.where(is_last[:n], 0.0, rolled(v, Z - 1)))
        return (source + BETA * beside) * scale

    def sweep1(first, last):
        def plane(p, _):
            for r in range(first + 8, last + 8, 16):
                sm1[p, r:r + 16, :] = smoothed(grad, p, grad[p, r:r + 16, :], r, 16)
            return 0

        if first < last:
            lax.fori_loop(1, X + 3, plane, 0)

    def sweep2(first, last):
        def plane(p, _):
            for r in range(first + 8, last + 8, 16):
                out[p - 2, r - 8:r + 8, :] = smoothed(sm1, p, grad[p, r:r + 16, :], r, 16)
            return 0

        if first < last:
            lax.fori_loop(2, X + 2, plane, 0)

    keep_low = jnp.where(low, 0.0, 1.0)
    keep_high = jnp.where(high, 0.0, 1.0)

    def sweep1_rows(p, _):
        for r, keep in ((7, keep_low), (R + 8, keep_high)):
            v = grad[p, r:r + 1, :]
            wide = jnp.broadcast_to(v, (8, Z))
            beside = (grad[p - 1, r:r + 1, :] + grad[p + 1, r:r + 1, :]
                      + grad[p, r - 1:r, :] + grad[p, r + 1:r + 2, :]
                      + (jnp.where(is_first[:8], 0.0, rolled(wide, 1))
                         + jnp.where(is_last[:8], 0.0, rolled(wide, Z - 1)))[0:1])
            sm1[p, r:r + 1, :] = (v + BETA * beside) * scale * keep
        return 0

    @pl.when(low)
    def _():
        grad[:, 0:8, :] = jnp.zeros((X + 4, 8, Z), jnp.float32)

    @pl.when(high)
    def _():
        grad[:, R + 8:R + 16, :] = jnp.zeros((X + 4, 8, Z), jnp.float32)

    done1, done2 = 16, 32
    for ci in range(C):
        gather(jnp.int32(ci))
        if ci == 0:
            @pl.when(jnp.logical_not(low))
            def _():
                for cp in row_copies(False):
                    cp.start()

        if ci == C - 1:
            @pl.when(jnp.logical_not(high))
            def _():
                for cp in row_copies(True):
                    cp.start()

        if ci >= 1:
            for side in range(2):
                g_remote(jnp.int32(ci - 1), side).wait_recv()
            upto = max(done1, ci * CH - 16)
            sweep1(done1, upto)
            done1 = upto
            upto = max(done2, ci * CH - 32)
            sweep2(done2, upto)
            done2 = upto

    for side in range(2):
        g_remote(jnp.int32(C - 1), side).wait_recv()

    @pl.when(jnp.logical_not(low))
    def _():
        for cp in row_copies(True):
            cp.wait_recv()

    @pl.when(jnp.logical_not(high))
    def _():
        for cp in row_copies(False):
            cp.wait_recv()

    sweep1(0, 16)
    sweep1(done1, R)
    lax.fori_loop(2, X + 2, sweep1_rows, 0)
    sweep2(0, 32)
    sweep2(done2, R)

    def drain(s, _):
        for side in range(2):
            lf_remote(s, side).wait_send()
            a_remote(s, side).wait_send()

        @pl.when(piece_of(s) != node)
        def _():
            for cp in q_copies(s):
                cp.wait_send()

        return 0

    lax.fori_loop(0, NC, drain, 0)

    def halo_drain(ci, _):
        for side in range(2):
            g_remote(ci, side).wait_send()
        return 0

    lax.fori_loop(0, C, halo_drain, 0)

    @pl.when(jnp.logical_not(high))
    def _():
        for cp in row_copies(True):
            cp.wait_send()

    @pl.when(jnp.logical_not(low))
    def _():
        for cp in row_copies(False):
            cp.wait_send()


def per_device(G, K, CH, logfield, state, target, node_index, weight_numer):
    X, Y, Z = target.shape
    R = Y // K
    CH = min(CH, R)
    C = R // CH
    NC = K * C
    f32, dma = jnp.float32, pltpu.SemaphoreType.DMA
    anywhere = pl.BlockSpec(memory_space=pl.ANY)
    scalars = pl.BlockSpec(memory_space=pltpu.SMEM)
    return pl.pallas_call(
        functools.partial(kernel, G, K, X, Y, Z, CH),
        out_shape=jax.ShapeDtypeStruct((X, R, Z), f32),
        in_specs=[anywhere, anywhere, anywhere, scalars, scalars],
        out_specs=pl.BlockSpec(memory_space=pltpu.VMEM),
        scratch_shapes=[
            pltpu.VMEM((NC, X + 2, CH + 64, Z), jnp.bfloat16),
            pltpu.VMEM((2, X, CH + 32, Z), f32),
            pltpu.VMEM((2, X, CH + 32, Z), f32),
            pltpu.VMEM((2, X + 2, CH + 64, Z), f32),
            pltpu.VMEM((2, X + 2, CH + 32, Z), f32),
            pltpu.VMEM((2, X, CH + 32, Z), f32),
            pltpu.VMEM((NC, 2, CH, Z), f32),
            pltpu.VMEM((NC, 2, CH, Z), f32),
            pltpu.VMEM((LAG + 1, X, CH, Z), f32),
            pltpu.VMEM((NC, X, CH, Z), jnp.int16),
            pltpu.VMEM((NC, 8, Z), f32),
            pltpu.VMEM((K + 1, C, X, CH, Z), jnp.int16),
            pltpu.VMEM((K + 1, C, 8, Z), f32),
            pltpu.VMEM((X + 4, R + 16, Z), f32),
            pltpu.VMEM((X + 4, R + 16, Z), f32),
            dma((NC,)), dma((2, NC)), dma((2, NC)), dma((2,)), dma((2,)), dma((2, NC)), dma((2, NC)),
            dma((NC,)), dma((K + 1, C)), dma((NC,)), dma((K + 1, C)), dma((2, C)), dma((2, C)), dma((6,)), dma((6,)),
        ],
        compiler_params=pltpu.CompilerParams(
            collective_id=0, has_side_effects=True, vmem_limit_bytes=58 * 1024 * 1024),
    )(logfield, state, target, node_index, weight_numer)


def solution(mesh):
    in_specs = (
        P("node", "gx", None, None),
        P("node", "gx", None, None),
        P("gx", None, None),
        P("node"),
        P("node"),
    )
    return jax.shard_map(
        functools.partial(per_device, mesh.shape["gx"], mesh.shape["node"], 64), mesh=mesh,
        in_specs=in_specs, out_specs=P("gx", "node", None), check_vma=False)
```

```python
import functools
import math

import jax
import jax.numpy as jnp
from jax import lax
from jax.experimental import pallas as pl
from jax.experimental.pallas import tpu as pltpu
from jax.sharding import PartitionSpec as P

RELAX = 2.0 / 3.0
BETA = 1.0
TOP = 32767.0
LAG = 2
MESH = pl.DeviceIdType.MESH


def rolled(v, by):
    return pltpu.roll(v, by, 1)


def kernel(G, K, X, Y, Z, CH, lf, st, tg, ni, wn, out,
           lfw, stw, tgw, kap, adj, inv, asend, ahalo, term, qs, sc, qr, sr, grad, sm1,
           lf_loc, lf_send, lf_recv, st_sem, tg_sem, a_send, a_recv,
           q_send, q_recv, s_send, s_recv, g_send, g_recv, r_send, r_recv):
    R = Y // K
    C = R // CH
    NC = K * C
    gx = lax.axis_index("gx")
    node = lax.axis_index("node")
    left = lax.rem(gx + G - 1, G)
    right = lax.rem(gx + 1, G)

    barrier = pltpu.get_barrier_semaphore()
    for k in range(K):
        for g in (left, right):
            pl.semaphore_signal(barrier, inc=1, device_id=(g, jnp.int32(k)), device_id_type=MESH)
    for k in range(1, K):
        pl.semaphore_signal(barrier, inc=1, device_id=(gx, lax.rem(node + k, K)), device_id_type=MESH)

    inner = (node > 0) & (node < K - 1)
    lag = jnp.where(inner, LAG, 0)
    orders = [sorted(range(K), key=lambda d: (-abs(d - p) if d != p else 1, -d)) for p in range(K)]
    turns = []
    for i in range(K):
        turn = jnp.int32(orders[0][i])
        for p in range(1, K):
            turn = jnp.where(node == p, orders[p][i], turn)
        turns.append(turn)

    def piece_of(s):
        i = s // C
        piece = turns[0]
        for n in range(1, K):
            piece = jnp.where(i == n, turns[n], piece)
        return piece

    def chunk_of(s):
        return piece_of(s) * C + lax.rem(s, C)

    def lf_start(s):
        first = chunk_of(s) * CH
        start = pl.multiple_of(jnp.clip(first - 16, 0, Y - CH - 32), 16)
        dst = pl.multiple_of(32 + start - first, 16)
        return start, dst

    def lf_local(s):
        start, dst = lf_start(s)
        return pltpu.make_async_copy(
            lf.at[0, :, pl.ds(start, CH + 32), :],
            lfw.at[s, pl.ds(1, X), pl.ds(dst, CH + 32), :], lf_loc.at[s])

    def lf_remote(s, side):
        start, dst = lf_start(s)
        src = 0 if side == 1 else X - 1
        to = X + 1 if side == 1 else 0
        return pltpu.make_async_remote_copy(
            src_ref=lf.at[0, src, pl.ds(start, CH + 32), :],
            dst_ref=lfw.at[s, to, pl.ds(dst, CH + 32), :],
            send_sem=lf_send.at[side, s], recv_sem=lf_recv.at[side, s],
            device_id=(left if side == 1 else right, node), device_id_type=MESH)

    def st_copies(s):
        first = chunk_of(s) * CH
        start = pl.multiple_of(jnp.clip(first - 8, 0, Y - CH - 16), 8)
        dst = pl.multiple_of(16 + start - first, 8)
        slot = lax.rem(s, 2)
        return (
            pltpu.make_async_copy(st.at[0, :, pl.ds(start, CH + 16), :],
                                  stw.at[slot, :, pl.ds(dst, CH + 16), :], st_sem.at[slot]),
            pltpu.make_async_copy(tg.at[:, pl.ds(start, CH + 16), :],
                                  tgw.at[slot, :, pl.ds(dst, CH + 16), :], tg_sem.at[slot]))

    def a_remote(s, side):
        return pltpu.make_async_remote_copy(
            src_ref=asend.at[s, 0 if side == 1 else 1],
            dst_ref=ahalo.at[s, side],
            send_sem=a_send.at[side, s], recv_sem=a_recv.at[side, s],
            device_id=(left if side == 1 else right, node), device_id_type=MESH)

    def q_copies(s):
        dest = piece_of(s)
        ci = lax.rem(s, C)
        upward = dest > node
        slot = jnp.where(dest == node - 1, K, dest)
        to = jnp.clip(jnp.where(upward, node + 1, node - 1), 0, K - 1)
        return (
            pltpu.make_async_remote_copy(
                src_ref=qs.at[s], dst_ref=qr.at[slot, ci], send_sem=q_send.at[s],
                recv_sem=q_recv.at[slot, ci], device_id=(gx, to), device_id_type=MESH),
            pltpu.make_async_remote_copy(
                src_ref=sc.at[s], dst_ref=sr.at[slot, ci], send_sem=s_send.at[s],
                recv_sem=s_recv.at[slot, ci], device_id=(gx, to), device_id_type=MESH))

    index = ni[0]
    half = jnp.float32(0.5 * math.cos(0.0))
    for i in range(1, 9):
        half = jnp.where(index == i, jnp.float32(0.5 * math.cos(math.pi * i / 8)), half)
    weight = wn[0].astype(jnp.float32) / 8.0
    lane = lax.broadcasted_iota(jnp.int32, (16, Z), 1)
    is_first = lane == 0
    is_last = lane == Z - 1

    for s in range(2):
        lf_local(s).start()
    for cp in st_copies(0):
        cp.start()
    pl.semaphore_wait(barrier, 3 * K - 1)
    for s in range(2):
        for side in range(2):
            lf_remote(s, side).start()

    def arrived(slot, ci):
        pltpu.make_async_remote_copy(
            src_ref=qs.at[0], dst_ref=qr.at[slot, ci], send_sem=q_send.at[0],
            recv_sem=q_recv.at[slot, ci], device_id=(left, node), device_id_type=MESH).wait_recv()
        pltpu.make_async_remote_copy(
            src_ref=sc.at[0], dst_ref=sr.at[slot, ci], send_sem=s_send.at[0],
            recv_sem=s_recv.at[slot, ci], device_id=(left, node), device_id_type=MESH).wait_recv()

    def phase1(s):
        slot = lax.rem(s, 2)
        c = chunk_of(s)

        @pl.when(s + 1 < NC)
        def _():
            for cp in st_copies(s + 1):
                cp.start()

        lf_local(s).wait()
        for side in range(2):
            lf_remote(s, side).wait_recv()

        def kappa(p, _):
            for r in range(16, CH + 48, 16):
                kap[slot, p, r:r + 16, :] = jnp.exp(half * lfw[s, p, r:r + 16, :].astype(jnp.float32))
            return 0

        lax.fori_loop(0, X + 2, kappa, 0)

        @pl.when(c == 0)
        def _():
            for p in range(1, X + 1):
                kap[slot, p, 31:32, :] = kap[slot, p, 32:33, :]

        @pl.when(c == NC - 1)
        def _():
            for p in range(1, X + 1):
                kap[slot, p, CH + 32:CH + 33, :] = kap[slot, p, CH + 31:CH + 32, :]

        for cp in st_copies(s):
            cp.wait()

        def first(p, _):
            for r in range(8, CH + 24, 16):
                j = r + 16
                k = kap[slot, p + 1, j:j + 16, :]
                total = (6.0 * k + kap[slot, p, j:j + 16, :] + kap[slot, p + 2, j:j + 16, :]
                         + kap[slot, p + 1, j - 1:j + 15, :] + kap[slot, p + 1, j + 1:j + 17, :]
                         + jnp.where(is_first, k, rolled(k, 1)) + jnp.where(is_last, k, rolled(k, Z - 1)))
                over = 1.0 / total
                inv[slot, p, r:r + 16, :] = over
                adj[slot, p + 1, r:r + 16, :] = (2.0 * RELAX) * (
                    stw[slot, p, r:r + 16, :] - tgw[slot, p, r:r + 16, :]) * over
            return 0

        lax.fori_loop(0, X, first, 0)

        asend[s, 0] = adj[slot, 1, 16:CH + 16, :]
        asend[s, 1] = adj[slot, X, 16:CH + 16, :]
        for side in range(2):
            a_remote(s, side).start()

        @pl.when(s + 2 < NC)
        def _():
            lf_local(s + 2).start()
            for side in range(2):
                lf_remote(s + 2, side).start()

        @pl.when(c == 0)
        def _():
            for p in range(1, X + 1):
                adj[slot, p, 15:16, :] = jnp.zeros((1, Z), jnp.float32)

        @pl.when(c == NC - 1)
        def _():
            for p in range(1, X + 1):
                adj[slot, p, CH + 16:CH + 17, :] = jnp.zeros((1, Z), jnp.float32)

    def phase2(s):
        slot = lax.rem(s, 2)
        place = lax.rem(s, LAG + 1)
        for side in range(2):
            a_remote(s, side).wait_recv()
        adj[slot, 0, 16:CH + 16, :] = ahalo[s, 0]
        adj[slot, X + 1, 16:CH + 16, :] = ahalo[s, 1]

        def second(p, _):
            for r in range(16, CH + 16, 16):
                j = r + 16
                k = kap[slot, p + 1, j:j + 16, :]
                a = adj[slot, p + 1, r:r + 16, :]
                ka = k * a
                am, ap = adj[slot, p, r:r + 16, :], adj[slot, p + 2, r:r + 16, :]
                bm, bp = adj[slot, p + 1, r - 1:r + 15, :], adj[slot, p + 1, r + 1:r + 17, :]
                beside = (am + ap + bm + bp
                          + jnp.where(is_first, 0.0, rolled(a, 1)) + jnp.where(is_last, 0.0, rolled(a, Z - 1)))
                beside_k = (kap[slot, p, j:j + 16, :] * am + kap[slot, p + 2, j:j + 16, :] * ap
                            + kap[slot, p + 1, j - 1:j + 15, :] * bm + kap[slot, p + 1, j + 1:j + 17, :] * bp
                            + jnp.where(is_first, 0.0, rolled(ka, 1)) + jnp.where(is_last, 0.0, rolled(ka, Z - 1)))
                t = (2.0 * RELAX) * weight * a + (RELAX * weight) * (k * beside + beside_k) * inv[slot, p, r:r + 16, :]
                term[place, p, r - 16:r, :] = t
            return 0

        lax.fori_loop(0, X, second, 0)

    def phase3(s):
        place = lax.rem(s, LAG + 1)
        dest = piece_of(s)
        ci = lax.rem(s, C)

        @pl.when((dest != node) & inner)
        def _():
            arrived(dest, ci)

            def add(p, _):
                for g in range(CH // 16):
                    rows = slice(g * 16, g * 16 + 16)
                    term[place, p, rows, :] += qr[dest, ci, p, rows, :].astype(jnp.float32) * sr[dest, ci, g:g + 1, :]
                return 0

            lax.fori_loop(0, X, add, 0)

        @pl.when(dest == node)
        def _():
            row = pl.multiple_of(8 + lax.rem(s, C) * CH, 8)
            for p in range(X):
                grad[2 + p, pl.ds(row, CH), :] = term[place, p]

        @pl.when(dest != node)
        def _():
            for g in range(CH // 16):
                most = jnp.abs(term[place, 0, g * 16:g * 16 + 16, :])
                for p in range(1, X):
                    most = jnp.maximum(most, jnp.abs(term[place, p, g * 16:g * 16 + 16, :]))
                most = jnp.maximum(jnp.max(most, axis=0, keepdims=True), 1e-20)
                sc[s, g:g + 1, :] = most * (1.0 / TOP)
                up = jnp.broadcast_to(TOP / most, (16, Z))
                for p in range(X):
                    q = jnp.round(term[place, p, g * 16:g * 16 + 16, :] * up)
                    qs[s, p, g * 16:g * 16 + 16, :] = q.astype(jnp.int32).astype(jnp.int16)
            for cp in q_copies(s):
                cp.start()

    def step(s, _):
        @pl.when(s < NC)
        def _():
            phase1(s)

        @pl.when((s >= 1) & (s < NC + 1))
        def _():
            phase2(s - 1)

        @pl.when((s >= 1 + lag) & (s < NC + 1 + lag))
        def _():
            phase3(s - 1 - lag)

        return 0

    lax.fori_loop(0, NC + 1 + LAG, step, 0)

    low, high = node == 0, node == K - 1

    def g_remote(ci, side):
        row = pl.multiple_of(8 + ci * CH, 8)
        return pltpu.make_async_remote_copy(
            src_ref=grad.at[pl.ds(2 if side == 1 else X, 2), pl.ds(row, CH), :],
            dst_ref=grad.at[pl.ds(X + 2 if side == 1 else 0, 2), pl.ds(row, CH), :],
            send_sem=g_send.at[side, ci], recv_sem=g_recv.at[side, ci],
            device_id=(left if side == 1 else right, node), device_id_type=MESH)

    def row_copies(up):
        src_row, dst_row, base = (R, 0, 0) if up else (8, R + 8, 3)
        to = jnp.clip(node + (1 if up else -1), 0, K - 1)
        result = []
        for n, (src, dst, count, g) in enumerate((
                (2, 2, X, gx), (2, X + 2, 1, left), (X + 1, 1, 1, right))):
            result.append(pltpu.make_async_remote_copy(
                src_ref=grad.at[pl.ds(src, count), pl.ds(src_row, 8), :],
                dst_ref=grad.at[pl.ds(dst, count), pl.ds(dst_row, 8), :],
                send_sem=r_send.at[base + n], recv_sem=r_recv.at[base + n],
                device_id=(g, to), device_id_type=MESH))
        return result

    def gather(ci):
        def add(slot):
            arrived(slot, ci)

            def plane(p, _):
                for g in range(CH // 16):
                    row = pl.multiple_of(8 + ci * CH + g * 16, 8)
                    grad[2 + p, pl.ds(row, 16), :] += (
                        qr[slot, ci, p, g * 16:g * 16 + 16, :].astype(jnp.float32) * sr[slot, ci, g:g + 1, :])
                return 0

            lax.fori_loop(0, X, plane, 0)

        @pl.when(node > 0)
        def _():
            add(node)

        @pl.when(node < K - 1)
        def _():
            add(jnp.int32(K))

        for side in range(2):
            g_remote(ci, side).start()

    scale = 1.0 / (1.0 + 6.0 * BETA)

    def smoothed(ref, p, source, r, n):
        v = ref[p, r:r + n, :]
        beside = (ref[p - 1, r:r + n, :] + ref[p + 1, r:r + n, :]
                  + ref[p, r - 1:r + n - 1, :] + ref[p, r + 1:r + n + 1, :]
                  + jnp.where(is_first[:n], 0.0, rolled(v, 1)) + jnp.where(is_last[:n], 0.0, rolled(v, Z - 1)))
        return (source + BETA * beside) * scale

    def sweep1(first, last):
        def plane(p, _):
            for r in range(first + 8, last + 8, 16):
                sm1[p, r:r + 16, :] = smoothed(grad, p, grad[p, r:r + 16, :], r, 16)
            return 0

        if first < last:
            lax.fori_loop(1, X + 3, plane, 0)

    def sweep2(first, last):
        def plane(p, _):
            for r in range(first + 8, last + 8, 16):
                out[p - 2, r - 8:r + 8, :] = smoothed(sm1, p, grad[p, r:r + 16, :], r, 16)
            return 0

        if first < last:
            lax.fori_loop(2, X + 2, plane, 0)

    keep_low = jnp.where(low, 0.0, 1.0)
    keep_high = jnp.where(high, 0.0, 1.0)

    def sweep1_rows(p, _):
        for r, keep in ((7, keep_low), (R + 8, keep_high)):
            v = grad[p, r:r + 1, :]
            wide = jnp.broadcast_to(v, (8, Z))
            beside = (grad[p - 1, r:r + 1, :] + grad[p + 1, r:r + 1, :]
                      + grad[p, r - 1:r, :] + grad[p, r + 1:r + 2, :]
                      + (jnp.where(is_first[:8], 0.0, rolled(wide, 1))
                         + jnp.where(is_last[:8], 0.0, rolled(wide, Z - 1)))[0:1])
            sm1[p, r:r + 1, :] = (v + BETA * beside) * scale * keep
        return 0

    @pl.when(low)
    def _():
        grad[:, 0:8, :] = jnp.zeros((X + 4, 8, Z), jnp.float32)

    @pl.when(high)
    def _():
        grad[:, R + 8:R + 16, :] = jnp.zeros((X + 4, 8, Z), jnp.float32)

    done1, done2 = 16, 32
    for ci in range(C):
        gather(jnp.int32(ci))
        if ci == 0:
            @pl.when(jnp.logical_not(low))
            def _():
                for cp in row_copies(False):
                    cp.start()

        if ci == C - 1:
            @pl.when(jnp.logical_not(high))
            def _():
                for cp in row_copies(True):
                    cp.start()

        if ci >= 1:
            for side in range(2):
                g_remote(jnp.int32(ci - 1), side).wait_recv()
            upto = max(done1, ci * CH - 16)
            sweep1(done1, upto)
            done1 = upto
            upto = max(done2, ci * CH - 32)
            sweep2(done2, upto)
            done2 = upto

    for side in range(2):
        g_remote(jnp.int32(C - 1), side).wait_recv()

    @pl.when(jnp.logical_not(low))
    def _():
        for cp in row_copies(True):
            cp.wait_recv()

    @pl.when(jnp.logical_not(high))
    def _():
        for cp in row_copies(False):
            cp.wait_recv()

    sweep1(0, 16)
    sweep1(done1, R)
    lax.fori_loop(2, X + 2, sweep1_rows, 0)
    sweep2(0, 32)
    sweep2(done2, R)

    def drain(s, _):
        for side in range(2):
            lf_remote(s, side).wait_send()
            a_remote(s, side).wait_send()

        @pl.when(piece_of(s) != node)
        def _():
            for cp in q_copies(s):
                cp.wait_send()

        return 0

    lax.fori_loop(0, NC, drain, 0)

    def halo_drain(ci, _):
        for side in range(2):
            g_remote(ci, side).wait_send()
        return 0

    lax.fori_loop(0, C, halo_drain, 0)

    @pl.when(jnp.logical_not(high))
    def _():
        for cp in row_copies(True):
            cp.wait_send()

    @pl.when(jnp.logical_not(low))
    def _():
        for cp in row_copies(False):
            cp.wait_send()


def per_device(G, K, CH, logfield, state, target, node_index, weight_numer):
    X, Y, Z = target.shape
    R = Y // K
    CH = min(CH, R)
    C = R // CH
    NC = K * C
    f32, dma = jnp.float32, pltpu.SemaphoreType.DMA
    anywhere = pl.BlockSpec(memory_space=pl.ANY)
    scalars = pl.BlockSpec(memory_space=pltpu.SMEM)
    return pl.pallas_call(
        functools.partial(kernel, G, K, X, Y, Z, CH),
        out_shape=jax.ShapeDtypeStruct((X, R, Z), f32),
        in_specs=[anywhere, anywhere, anywhere, scalars, scalars],
        out_specs=pl.BlockSpec(memory_space=pltpu.VMEM),
        scratch_shapes=[
            pltpu.VMEM((NC, X + 2, CH + 64, Z), jnp.bfloat16),
            pltpu.VMEM((2, X, CH + 32, Z), f32),
            pltpu.VMEM((2, X, CH + 32, Z), f32),
            pltpu.VMEM((2, X + 2, CH + 64, Z), f32),
            pltpu.VMEM((2, X + 2, CH + 32, Z), f32),
            pltpu.VMEM((2, X, CH + 32, Z), f32),
            pltpu.VMEM((NC, 2, CH, Z), f32),
            pltpu.VMEM((NC, 2, CH, Z), f32),
            pltpu.VMEM((LAG + 1, X, CH, Z), f32),
            pltpu.VMEM((NC, X, CH, Z), jnp.int16),
            pltpu.VMEM((NC, 8, Z), f32),
            pltpu.VMEM((K + 1, C, X, CH, Z), jnp.int16),
            pltpu.VMEM((K + 1, C, 8, Z), f32),
            pltpu.VMEM((X + 4, R + 16, Z), f32),
            pltpu.VMEM((X + 4, R + 16, Z), f32),
            dma((NC,)), dma((2, NC)), dma((2, NC)), dma((2,)), dma((2,)), dma((2, NC)), dma((2, NC)),
            dma((NC,)), dma((K + 1, C)), dma((NC,)), dma((K + 1, C)), dma((2, C)), dma((2, C)), dma((6,)), dma((6,)),
        ],
        compiler_params=pltpu.CompilerParams(
            collective_id=0, has_side_effects=True, vmem_limit_bytes=58 * 1024 * 1024),
    )(logfield, state, target, node_index, weight_numer)


def solution(mesh):
    in_specs = (
        P("node", "gx", None, None),
        P("node", "gx", None, None),
        P("gx", None, None),
        P("node"),
        P("node"),
    )
    return jax.shard_map(
        functools.partial(per_device, mesh.shape["gx"], mesh.shape["node"], 64), mesh=mesh,
        in_specs=in_specs, out_specs=P("gx", "node", None), check_vma=False)
```

```python
import functools
import math

import jax
import jax.numpy as jnp
from jax import lax
from jax.experimental import pallas as pl
from jax.experimental.pallas import tpu as pltpu
from jax.sharding import PartitionSpec as P

RELAX = 2.0 / 3.0
BETA = 1.0
TOP = 32767.0
LAG = 2
MESH = pl.DeviceIdType.MESH


def rolled(v, by):
    return pltpu.roll(v, by, 1)


def kernel(G, K, X, Y, Z, CH, lf, st, tg, ni, wn, out,
           lfw, stw, tgw, kap, adj, inv, asend, ahalo, term, qs, sc, qr, sr, grad, sm1,
           lf_loc, lf_send, lf_recv, st_sem, tg_sem, a_send, a_recv,
           q_send, q_recv, s_send, s_recv, g_send, g_recv, r_send, r_recv):
    R = Y // K
    C = R // CH
    NC = K * C
    gx = lax.axis_index("gx")
    node = lax.axis_index("node")
    left = lax.rem(gx + G - 1, G)
    right = lax.rem(gx + 1, G)

    barrier = pltpu.get_barrier_semaphore()
    for k in range(K):
        for g in (left, right):
            pl.semaphore_signal(barrier, inc=1, device_id=(g, jnp.int32(k)), device_id_type=MESH)
    for k in range(1, K):
        pl.semaphore_signal(barrier, inc=1, device_id=(gx, lax.rem(node + k, K)), device_id_type=MESH)

    inner = (node > 0) & (node < K - 1)
    lag = jnp.where(inner, LAG, 0)
    orders = [sorted(range(K), key=lambda d: (-abs(d - p) if d != p else 1, -abs(2 * d - K + 1))) for p in range(K)]
    turns = []
    for i in range(K):
        turn = jnp.int32(orders[0][i])
        for p in range(1, K):
            turn = jnp.where(node == p, orders[p][i], turn)
        turns.append(turn)

    def piece_of(s):
        i = s // C
        piece = turns[0]
        for n in range(1, K):
            piece = jnp.where(i == n, turns[n], piece)
        return piece

    def chunk_of(s):
        return piece_of(s) * C + lax.rem(s, C)

    def lf_start(s):
        first = chunk_of(s) * CH
        start = pl.multiple_of(jnp.clip(first - 16, 0, Y - CH - 32), 16)
        dst = pl.multiple_of(32 + start - first, 16)
        return start, dst

    def lf_local(s):
        start, dst = lf_start(s)
        return pltpu.make_async_copy(
            lf.at[0, :, pl.ds(start, CH + 32), :],
            lfw.at[s, pl.ds(1, X), pl.ds(dst, CH + 32), :], lf_loc.at[s])

    def lf_remote(s, side):
        start, dst = lf_start(s)
        src = 0 if side == 1 else X - 1
        to = X + 1 if side == 1 else 0
        return pltpu.make_async_remote_copy(
            src_ref=lf.at[0, src, pl.ds(start, CH + 32), :],
            dst_ref=lfw.at[s, to, pl.ds(dst, CH + 32), :],
            send_sem=lf_send.at[side, s], recv_sem=lf_recv.at[side, s],
            device_id=(left if side == 1 else right, node), device_id_type=MESH)

    def st_copies(s):
        first = chunk_of(s) * CH
        start = pl.multiple_of(jnp.clip(first - 8, 0, Y - CH - 16), 8)
        dst = pl.multiple_of(16 + start - first, 8)
        slot = lax.rem(s, 2)
        return (
            pltpu.make_async_copy(st.at[0, :, pl.ds(start, CH + 16), :],
                                  stw.at[slot, :, pl.ds(dst, CH + 16), :], st_sem.at[slot]),
            pltpu.make_async_copy(tg.at[:, pl.ds(start, CH + 16), :],
                                  tgw.at[slot, :, pl.ds(dst, CH + 16), :], tg_sem.at[slot]))

    def a_remote(s, side):
        return pltpu.make_async_remote_copy(
            src_ref=asend.at[s, 0 if side == 1 else 1],
            dst_ref=ahalo.at[s, side],
            send_sem=a_send.at[side, s], recv_sem=a_recv.at[side, s],
            device_id=(left if side == 1 else right, node), device_id_type=MESH)

    def q_copies(s):
        dest = piece_of(s)
        ci = lax.rem(s, C)
        upward = dest > node
        slot = jnp.where(dest == node - 1, K, dest)
        to = jnp.clip(jnp.where(upward, node + 1, node - 1), 0, K - 1)
        return (
            pltpu.make_async_remote_copy(
                src_ref=qs.at[s], dst_ref=qr.at[slot, ci], send_sem=q_send.at[s],
                recv_sem=q_recv.at[slot, ci], device_id=(gx, to), device_id_type=MESH),
            pltpu.make_async_remote_copy(
                src_ref=sc.at[s], dst_ref=sr.at[slot, ci], send_sem=s_send.at[s],
                recv_sem=s_recv.at[slot, ci], device_id=(gx, to), device_id_type=MESH))

    index = ni[0]
    half = jnp.float32(0.5 * math.cos(0.0))
    for i in range(1, 9):
        half = jnp.where(index == i, jnp.float32(0.5 * math.cos(math.pi * i / 8)), half)
    weight = wn[0].astype(jnp.float32) / 8.0
    lane = lax.broadcasted_iota(jnp.int32, (16, Z), 1)
    is_first = lane == 0
    is_last = lane == Z - 1

    for s in range(2):
        lf_local(s).start()
    for cp in st_copies(0):
        cp.start()
    pl.semaphore_wait(barrier, 3 * K - 1)
    for s in range(2):
        for side in range(2):
            lf_remote(s, side).start()

    def arrived(slot, ci):
        pltpu.make_async_remote_copy(
            src_ref=qs.at[0], dst_ref=qr.at[slot, ci], send_sem=q_send.at[0],
            recv_sem=q_recv.at[slot, ci], device_id=(left, node), device_id_type=MESH).wait_recv()
        pltpu.make_async_remote_copy(
            src_ref=sc.at[0], dst_ref=sr.at[slot, ci], send_sem=s_send.at[0],
            recv_sem=s_recv.at[slot, ci], device_id=(left, node), device_id_type=MESH).wait_recv()

    def phase1(s):
        slot = lax.rem(s, 2)
        c = chunk_of(s)

        @pl.when(s + 1 < NC)
        def _():
            for cp in st_copies(s + 1):
                cp.start()

        lf_local(s).wait()
        for side in range(2):
            lf_remote(s, side).wait_recv()

        def kappa(p, _):
            for r in range(16, CH + 48, 16):
                kap[slot, p, r:r + 16, :] = jnp.exp(half * lfw[s, p, r:r + 16, :].astype(jnp.float32))
            return 0

        lax.fori_loop(0, X + 2, kappa, 0)

        @pl.when(c == 0)
        def _():
            for p in range(1, X + 1):
                kap[slot, p, 31:32, :] = kap[slot, p, 32:33, :]

        @pl.when(c == NC - 1)
        def _():
            for p in range(1, X + 1):
                kap[slot, p, CH + 32:CH + 33, :] = kap[slot, p, CH + 31:CH + 32, :]

        for cp in st_copies(s):
            cp.wait()

        def first(p, _):
            for r in range(8, CH + 24, 16):
                j = r + 16
                k = kap[slot, p + 1, j:j + 16, :]
                total = (6.0 * k + kap[slot, p, j:j + 16, :] + kap[slot, p + 2, j:j + 16, :]
                         + kap[slot, p + 1, j - 1:j + 15, :] + kap[slot, p + 1, j + 1:j + 17, :]
                         + jnp.where(is_first, k, rolled(k, 1)) + jnp.where(is_last, k, rolled(k, Z - 1)))
                over = 1.0 / total
                inv[slot, p, r:r + 16, :] = over
                adj[slot, p + 1, r:r + 16, :] = (2.0 * RELAX) * (
                    stw[slot, p, r:r + 16, :] - tgw[slot, p, r:r + 16, :]) * over
            return 0

        lax.fori_loop(0, X, first, 0)

        asend[s, 0] = adj[slot, 1, 16:CH + 16, :]
        asend[s, 1] = adj[slot, X, 16:CH + 16, :]
        for side in range(2):
            a_remote(s, side).start()

        @pl.when(s + 2 < NC)
        def _():
            lf_local(s + 2).start()
            for side in range(2):
                lf_remote(s + 2, side).start()

        @pl.when(c == 0)
        def _():
            for p in range(1, X + 1):
                adj[slot, p, 15:16, :] = jnp.zeros((1, Z), jnp.float32)

        @pl.when(c == NC - 1)
        def _():
            for p in range(1, X + 1):
                adj[slot, p, CH + 16:CH + 17, :] = jnp.zeros((1, Z), jnp.float32)

    def phase2(s):
        slot = lax.rem(s, 2)
        place = lax.rem(s, LAG + 1)
        for side in range(2):
            a_remote(s, side).wait_recv()
        adj[slot, 0, 16:CH + 16, :] = ahalo[s, 0]
        adj[slot, X + 1, 16:CH + 16, :] = ahalo[s, 1]

        def second(p, _):
            for r in range(16, CH + 16, 16):
                j = r + 16
                k = kap[slot, p + 1, j:j + 16, :]
                a = adj[slot, p + 1, r:r + 16, :]
                ka = k * a
                am, ap = adj[slot, p, r:r + 16, :], adj[slot, p + 2, r:r + 16, :]
                bm, bp = adj[slot, p + 1, r - 1:r + 15, :], adj[slot, p + 1, r + 1:r + 17, :]
                beside = (am + ap + bm + bp
                          + jnp.where(is_first, 0.0, rolled(a, 1)) + jnp.where(is_last, 0.0, rolled(a, Z - 1)))
                beside_k = (kap[slot, p, j:j + 16, :] * am + kap[slot, p + 2, j:j + 16, :] * ap
                            + kap[slot, p + 1, j - 1:j + 15, :] * bm + kap[slot, p + 1, j + 1:j + 17, :] * bp
                            + jnp.where(is_first, 0.0, rolled(ka, 1)) + jnp.where(is_last, 0.0, rolled(ka, Z - 1)))
                t = (2.0 * RELAX) * weight * a + (RELAX * weight) * (k * beside + beside_k) * inv[slot, p, r:r + 16, :]
                term[place, p, r - 16:r, :] = t
            return 0

        lax.fori_loop(0, X, second, 0)

    def phase3(s):
        place = lax.rem(s, LAG + 1)
        dest = piece_of(s)
        ci = lax.rem(s, C)

        @pl.when((dest != node) & inner)
        def _():
            arrived(dest, ci)

            def add(p, _):
                for g in range(CH // 16):
                    rows = slice(g * 16, g * 16 + 16)
                    term[place, p, rows, :] += qr[dest, ci, p, rows, :].astype(jnp.float32) * sr[dest, ci, g:g + 1, :]
                return 0

            lax.fori_loop(0, X, add, 0)

        @pl.when(dest == node)
        def _():
            row = pl.multiple_of(8 + lax.rem(s, C) * CH, 8)
            for p in range(X):
                grad[2 + p, pl.ds(row, CH), :] = term[place, p]

        @pl.when(dest != node)
        def _():
            for g in range(CH // 16):
                most = jnp.abs(term[place, 0, g * 16:g * 16 + 16, :])
                for p in range(1, X):
                    most = jnp.maximum(most, jnp.abs(term[place, p, g * 16:g * 16 + 16, :]))
                most = jnp.maximum(jnp.max(most, axis=0, keepdims=True), 1e-20)
                sc[s, g:g + 1, :] = most * (1.0 / TOP)
                up = jnp.broadcast_to(TOP / most, (16, Z))
                for p in range(X):
                    q = jnp.round(term[place, p, g * 16:g * 16 + 16, :] * up)
                    qs[s, p, g * 16:g * 16 + 16, :] = q.astype(jnp.int32).astype(jnp.int16)
            for cp in q_copies(s):
                cp.start()

    def step(s, _):
        @pl.when(s < NC)
        def _():
            phase1(s)

        @pl.when((s >= 1) & (s < NC + 1))
        def _():
            phase2(s - 1)

        @pl.when((s >= 1 + lag) & (s < NC + 1 + lag))
        def _():
            phase3(s - 1 - lag)

        return 0

    lax.fori_loop(0, NC + 1 + LAG, step, 0)

    low, high = node == 0, node == K - 1

    def g_remote(ci, side):
        row = pl.multiple_of(8 + ci * CH, 8)
        return pltpu.make_async_remote_copy(
            src_ref=grad.at[pl.ds(2 if side == 1 else X, 2), pl.ds(row, CH), :],
            dst_ref=grad.at[pl.ds(X + 2 if side == 1 else 0, 2), pl.ds(row, CH), :],
            send_sem=g_send.at[side, ci], recv_sem=g_recv.at[side, ci],
            device_id=(left if side == 1 else right, node), device_id_type=MESH)

    def row_copies(up):
        src_row, dst_row, base = (R, 0, 0) if up else (8, R + 8, 3)
        to = jnp.clip(node + (1 if up else -1), 0, K - 1)
        result = []
        for n, (src, dst, count, g) in enumerate((
                (2, 2, X, gx), (2, X + 2, 1, left), (X + 1, 1, 1, right))):
            result.append(pltpu.make_async_remote_copy(
                src_ref=grad.at[pl.ds(src, count), pl.ds(src_row, 8), :],
                dst_ref=grad.at[pl.ds(dst, count), pl.ds(dst_row, 8), :],
                send_sem=r_send.at[base + n], recv_sem=r_recv.at[base + n],
                device_id=(g, to), device_id_type=MESH))
        return result

    def gather(ci):
        def add(slot):
            arrived(slot, ci)

            def plane(p, _):
                for g in range(CH // 16):
                    row = pl.multiple_of(8 + ci * CH + g * 16, 8)
                    grad[2 + p, pl.ds(row, 16), :] += (
                        qr[slot, ci, p, g * 16:g * 16 + 16, :].astype(jnp.float32) * sr[slot, ci, g:g + 1, :])
                return 0

            lax.fori_loop(0, X, plane, 0)

        @pl.when(node > 0)
        def _():
            add(node)

        @pl.when(node < K - 1)
        def _():
            add(jnp.int32(K))

        for side in range(2):
            g_remote(ci, side).start()

    scale = 1.0 / (1.0 + 6.0 * BETA)

    def smoothed(ref, p, source, r, n):
        v = ref[p, r:r + n, :]
        beside = (ref[p - 1, r:r + n, :] + ref[p + 1, r:r + n, :]
                  + ref[p, r - 1:r + n - 1, :] + ref[p, r + 1:r + n + 1, :]
                  + jnp.where(is_first[:n], 0.0, rolled(v, 1)) + jnp.where(is_last[:n], 0.0, rolled(v, Z - 1)))
        return (source + BETA * beside) * scale

    def sweep1(first, last):
        def plane(p, _):
            for r in range(first + 8, last + 8, 16):
                sm1[p, r:r + 16, :] = smoothed(grad, p, grad[p, r:r + 16, :], r, 16)
            return 0

        if first < last:
            lax.fori_loop(1, X + 3, plane, 0)

    def sweep2(first, last):
        def plane(p, _):
            for r in range(first + 8, last + 8, 16):
                out[p - 2, r - 8:r + 8, :] = smoothed(sm1, p, grad[p, r:r + 16, :], r, 16)
            return 0

        if first < last:
            lax.fori_loop(2, X + 2, plane, 0)

    keep_low = jnp.where(low, 0.0, 1.0)
    keep_high = jnp.where(high, 0.0, 1.0)

    def sweep1_rows(p, _):
        for r, keep in ((7, keep_low), (R + 8, keep_high)):
            v = grad[p, r:r + 1, :]
            wide = jnp.broadcast_to(v, (8, Z))
            beside = (grad[p - 1, r:r + 1, :] + grad[p + 1, r:r + 1, :]
                      + grad[p, r - 1:r, :] + grad[p, r + 1:r + 2, :]
                      + (jnp.where(is_first[:8], 0.0, rolled(wide, 1))
                         + jnp.where(is_last[:8], 0.0, rolled(wide, Z - 1)))[0:1])
            sm1[p, r:r + 1, :] = (v + BETA * beside) * scale * keep
        return 0

    @pl.when(low)
    def _():
        grad[:, 0:8, :] = jnp.zeros((X + 4, 8, Z), jnp.float32)

    @pl.when(high)
    def _():
        grad[:, R + 8:R + 16, :] = jnp.zeros((X + 4, 8, Z), jnp.float32)

    done1, done2 = 16, 32
    for ci in range(C):
        gather(jnp.int32(ci))
        if ci == 0:
            @pl.when(jnp.logical_not(low))
            def _():
                for cp in row_copies(False):
                    cp.start()

        if ci == C - 1:
            @pl.when(jnp.logical_not(high))
            def _():
                for cp in row_copies(True):
                    cp.start()

        if ci >= 1:
            for side in range(2):
                g_remote(jnp.int32(ci - 1), side).wait_recv()
            upto = max(done1, ci * CH - 16)
            sweep1(done1, upto)
            done1 = upto
            upto = max(done2, ci * CH - 32)
            sweep2(done2, upto)
            done2 = upto

    for side in range(2):
        g_remote(jnp.int32(C - 1), side).wait_recv()

    @pl.when(jnp.logical_not(low))
    def _():
        for cp in row_copies(True):
            cp.wait_recv()

    @pl.when(jnp.logical_not(high))
    def _():
        for cp in row_copies(False):
            cp.wait_recv()

    sweep1(0, 16)
    sweep1(done1, R)
    lax.fori_loop(2, X + 2, sweep1_rows, 0)
    sweep2(0, 32)
    sweep2(done2, R)

    def drain(s, _):
        for side in range(2):
            lf_remote(s, side).wait_send()
            a_remote(s, side).wait_send()

        @pl.when(piece_of(s) != node)
        def _():
            for cp in q_copies(s):
                cp.wait_send()

        return 0

    lax.fori_loop(0, NC, drain, 0)

    def halo_drain(ci, _):
        for side in range(2):
            g_remote(ci, side).wait_send()
        return 0

    lax.fori_loop(0, C, halo_drain, 0)

    @pl.when(jnp.logical_not(high))
    def _():
        for cp in row_copies(True):
            cp.wait_send()

    @pl.when(jnp.logical_not(low))
    def _():
        for cp in row_copies(False):
            cp.wait_send()


def per_device(G, K, CH, logfield, state, target, node_index, weight_numer):
    X, Y, Z = target.shape
    R = Y // K
    CH = min(CH, R)
    C = R // CH
    NC = K * C
    f32, dma = jnp.float32, pltpu.SemaphoreType.DMA
    anywhere = pl.BlockSpec(memory_space=pl.ANY)
    scalars = pl.BlockSpec(memory_space=pltpu.SMEM)
    return pl.pallas_call(
        functools.partial(kernel, G, K, X, Y, Z, CH),
        out_shape=jax.ShapeDtypeStruct((X, R, Z), f32),
        in_specs=[anywhere, anywhere, anywhere, scalars, scalars],
        out_specs=pl.BlockSpec(memory_space=pltpu.VMEM),
        scratch_shapes=[
            pltpu.VMEM((NC, X + 2, CH + 64, Z), jnp.bfloat16),
            pltpu.VMEM((2, X, CH + 32, Z), f32),
            pltpu.VMEM((2, X, CH + 32, Z), f32),
            pltpu.VMEM((2, X + 2, CH + 64, Z), f32),
            pltpu.VMEM((2, X + 2, CH + 32, Z), f32),
            pltpu.VMEM((2, X, CH + 32, Z), f32),
            pltpu.VMEM((NC, 2, CH, Z), f32),
            pltpu.VMEM((NC, 2, CH, Z), f32),
            pltpu.VMEM((LAG + 1, X, CH, Z), f32),
            pltpu.VMEM((NC, X, CH, Z), jnp.int16),
            pltpu.VMEM((NC, 8, Z), f32),
            pltpu.VMEM((K + 1, C, X, CH, Z), jnp.int16),
            pltpu.VMEM((K + 1, C, 8, Z), f32),
            pltpu.VMEM((X + 4, R + 16, Z), f32),
            pltpu.VMEM((X + 4, R + 16, Z), f32),
            dma((NC,)), dma((2, NC)), dma((2, NC)), dma((2,)), dma((2,)), dma((2, NC)), dma((2, NC)),
            dma((NC,)), dma((K + 1, C)), dma((NC,)), dma((K + 1, C)), dma((2, C)), dma((2, C)), dma((6,)), dma((6,)),
        ],
        compiler_params=pltpu.CompilerParams(
            collective_id=0, has_side_effects=True, vmem_limit_bytes=58 * 1024 * 1024),
    )(logfield, state, target, node_index, weight_numer)


def solution(mesh):
    in_specs = (
        P("node", "gx", None, None),
        P("node", "gx", None, None),
        P("gx", None, None),
        P("node"),
        P("node"),
    )
    return jax.shard_map(
        functools.partial(per_device, mesh.shape["gx"], mesh.shape["node"], 64), mesh=mesh,
        in_specs=in_specs, out_specs=P("gx", "node", None), check_vma=False)
```
